128 devices in a mesh: dp: 4 (over x_lo, core), expert: 32 (over z, y, x_hi).
Axes of the slice: x: 4 (x_hi: 2, x_lo: 2; x = x_hi * 2 + x_lo), y: 4, z: 4, core: 2. Of those that a mesh axis runs over, the one named last changes fastest.
Arguments:
- hidden: bfloat16 [131072, 8, 1536], P(('dp', 'expert')), may hold values from -96 to 96, as said below
- expert_ids: int32 [131072, 8], P(('dp', 'expert')), may hold values from 0 to 127, all different within a row; in each aligned block of 1024 rows (0 to 1023, 1024 to 2047, ...) at most 96 rows name the same one
Outputs:
- factors: float32 [32, 1536, 1536], P('expert', 'dp')
The draws below stay inside these ranges and needn't reach their ends.
Inputs may be any that keep to these rules, and one draw needn't show every extreme that they name: `hidden`: entries are real-valued activations. `expert_ids`: each token names 8 different experts; among the 1024 tokens of one device no expert is named by more than 96 tokens; every expert is named by some token.
All inputs are finite; a program needn't handle non-finite values.
Results may differ from the reference program's by a relative error of at most 0.0003.
Values may be sent and summed in bfloat16 or wider, within the bound.
No kernel may reach another device: no remote copies, remote signals or barrier semaphores. Data moves between devices by JAX's collectives and lax.ppermute only.
A program may use at most 192 MiB of HBM per device.

```python
import math
import jax
import jax.numpy as jnp
import numpy as np
from jax import lax

FF = 1536
TOP = 8
EXP_DEV = 4
TOK_DEV = 1024
EXPERTS = 128
TOKENS = 131072
CAP = 96


def draw_hidden(key, part):
    key = jax.random.fold_in(key, 11)
    key_a, key_b, key_c = jax.random.split(key, 3)
    spread = math.log(10.0)
    col_scale = 0.3 * jnp.exp(jax.random.uniform(key_b, (FF,), jnp.float32, 0.0, spread))
    row_scale = 0.3 * jnp.exp(jax.random.uniform(key_c, (TOKENS, TOP, 1), jnp.float32, 0.0, spread))
    ramp = jnp.arange(TOKENS, dtype=jnp.float32).reshape(TOKENS, 1, 1) / TOKENS
    base = jnp.clip(jax.random.normal(key_a, (TOKENS, TOP, FF), jnp.float32), -6.0, 6.0)
    values = base * jnp.exp(0.55 * ramp)
    return (values * row_scale * col_scale).astype(jnp.bfloat16)


def deal_out(stream_key, own, number, rows, number_of, top, reach, skew):
    order = jax.random.permutation(stream_key, number_of)
    heavy_load, common = load_shares(number_of, rows * top, reach, skew, True), load_shares(number_of, rows * top, reach, skew, False)
    places = jnp.arange(number_of)

    def named(sizes, offset_by):
        used = int((sizes > 0).sum())
        fixed = max(1, used // 4)
        shifted = fixed + (places - fixed + offset_by * (used - fixed)) % max(1, number_of - fixed)
        return jnp.zeros((number_of,), jnp.int32).at[order[jnp.where(places < fixed, places, shifted)]].set(jnp.asarray(sizes, jnp.int32))

    sizes = jnp.where(number % 4 == 0, named(heavy_load, number // 4), named(common, number - number // 4 - 1))
    mixed = jax.random.permutation(jax.random.fold_in(own, 3), number_of)
    giver, sink = mixed[0:number_of // 2 * 2:2], mixed[1:number_of // 2 * 2:2]
    slack = jnp.minimum(sizes[giver] - 1, reach - sizes[sink]) // 2
    slack = jnp.where((giver == order[0]) | (sink == order[0]) | (sizes[sink] == 0), 0, jnp.maximum(slack, 0))
    shifted = jax.random.randint(jax.random.fold_in(own, 4), (number_of // 2,), 0, 1 << 20) % (slack + 1)
    sizes = sizes.at[giver].add(-shifted).at[sink].add(shifted)
    members = jnp.searchsorted(jnp.cumsum(sizes), jnp.arange(rows * top), side="right").astype(jnp.int32)
    grid = members.reshape(top, rows).T
    grid = grid[jax.random.permutation(jax.random.fold_in(own, 1), rows)]
    offset_by = jax.random.randint(jax.random.fold_in(own, 2), (rows, 1), 0, top)
    return jnp.take_along_axis(grid, (jnp.arange(top)[None, :] + offset_by) % top, axis=1)


def load_shares(count, total, reach, skew, full):
    weights = [(1 << 20) // math.isqrt(grade ** skew) + 1 for grade in range(1, count + 1)]
    largest = reach if full else min(reach, max(-(-total // count), total * weights[0] // sum(weights)))
    least = 1 if total - largest >= count - 1 else 0
    given, surplus = [largest] + [least] * (count - 1), total - largest - least * (count - 1)
    while surplus > 0:
        movable = [i for i in range(1, count) if given[i] < largest] or [i for i in range(1, count) if given[i] < reach]
        whole, budget = sum([weights[i] for i in movable]), surplus
        for i in movable:
            more = min(reach - given[i], max(1, budget * weights[i] // whole), surplus)
            given[i] = given[i] + more
            surplus = surplus - more
    return np.array(given)


def setup_inputs(seed: int = 0) -> dict:
    seeds = jax.random.split(jax.random.key(seed), 3)
    hidden = draw_hidden(jax.random.fold_in(seeds[2], 71), 0)
    expert_ids_keys = jax.random.split(jax.random.fold_in(seeds[1], 1), TOKENS // TOK_DEV)
    expert_ids_turns = jax.random.permutation(jax.random.fold_in(seeds[1], 3), TOKENS // TOK_DEV)
    expert_ids = jax.vmap(lambda own, number: deal_out(jax.random.fold_in(seeds[1], 2), own, number, TOK_DEV, EXPERTS, TOP, CAP, 1))(expert_ids_keys, expert_ids_turns).reshape((TOKENS, TOP))
    return dict(hidden=hidden, expert_ids=expert_ids)


damp_share = 0.01

def reference(hidden, expert_ids):
    features = hidden.shape[2]
    row_data = hidden.reshape(-1, features)
    flat_ids = expert_ids.reshape(-1)
    owner_count = EXPERTS // EXP_DEV
    sort_keys = jnp.where(flat_ids % EXP_DEV == 0, flat_ids // EXP_DEV, owner_count).astype(jnp.int32)
    ordering = jnp.argsort(sort_keys, stable=True).astype(jnp.int32)
    owner_range = jnp.arange(owner_count, dtype=jnp.int32)
    counts = jnp.sum((sort_keys[:, None] == owner_range[None, :]).astype(jnp.int32), axis=0).astype(jnp.int32)
    starts = (jnp.cumsum(counts) - counts).astype(jnp.int32)
    most_rows = CAP * (TOKENS // TOK_DEV)
    total_rows = ordering.shape[0]

    def factor_one(pair):
        first_row, row_count = pair
        slot_index = jnp.arange(most_rows, dtype=jnp.int32)
        is_live = slot_index < row_count
        position = jnp.clip(first_row + slot_index, 0, total_rows - 1).astype(jnp.int32)
        picked = jnp.where(is_live, ordering[position], 0).astype(jnp.int32)
        picked_rows = jnp.where(is_live[:, None], row_data[picked].astype(jnp.float32), jnp.float32(0.0))
        gram_sum = jnp.dot(picked_rows.T.astype(jnp.float32), picked_rows.astype(jnp.float32), precision=lax.Precision.HIGHEST, preferred_element_type=jnp.float32)
        scaling = jnp.float32(2.0) / row_count.astype(jnp.float32)
        damping = damp_share * scaling * jnp.trace(gram_sum) / features
        damped = scaling * gram_sum + damping * jnp.eye(features, dtype=jnp.float32)
        return jnp.linalg.cholesky(damped)
    return lax.map(factor_one, (starts, counts))
```

```python
import functools

import jax
import jax.numpy as jnp
from jax import lax
from jax.experimental import pallas as pl
from jax.experimental.pallas import tpu as pltpu
from jax.sharding import PartitionSpec as P

EXP_DEV = 4
WIDTH = 128
damp_share = 0.01
f32 = jnp.float32
bf16 = jnp.bfloat16


def split(x):
    high = x.astype(bf16)
    rest = x - high.astype(f32)
    middle = rest.astype(bf16)
    return high, middle, (rest - middle.astype(f32)).astype(bf16)


def left_terms(x):
    h, m, l = split(x)
    return jnp.concatenate([h, h, m, m, h, l], 1)


def right_terms(x):
    h, m, l = split(x)
    return jnp.concatenate([h, m, h, m, l, h], 1)


def dot_nt(a, b):
    return lax.dot_general(a, b, (((1,), (1,)), ((), ())), preferred_element_type=f32)


def reciprocal(x):
    r = pl.reciprocal(x, approx=True)
    r = r * (2.0 - x * r)
    return r * (2.0 - x * r)


def over_lanes(x, j):
    return jnp.broadcast_to(x[:, j : j + 1], (8, 128))


def over_rows(x, i):
    return jnp.broadcast_to(x[i : i + 1, :], x.shape)


def eliminate(rows):
    count = len(rows)
    wide = lambda v: jnp.concatenate([v, v], axis=1)
    rows = list(rows)
    sub = lax.broadcasted_iota(jnp.int32, (8, 128), 0)
    for m in range(count):
        group = rows[m]
        cols = [over_lanes(group, 8 * m + l) for l in range(8)]
        cell = [[over_rows(cols[l], i) if i >= l else None for l in range(8)] for i in range(8)]
        below = [[over_lanes(rows[t], 8 * m + l) for l in range(8)] for t in range(m + 1, count)]
        inverse, pivots, diagonal = [], [], None
        for j in range(8):
            d = cell[j][j]
            r = reciprocal(d)
            inverse.append(r)
            diagonal = d if diagonal is None else jnp.where(sub == j, d, diagonal)
            pairs = [(i, l) for i in range(j + 1, 8) for l in range(j + 1, i + 1)]
            products = [cell[i][j] * cell[l][j] for i, l in pairs]
            for (i, l), product in zip(pairs, products):
                cell[i][l] = cell[i][l] - product * r
            pivot = over_rows(group, j)
            pivots.append(pivot)
            group = group - wide(jnp.where(sub > j, cols[j] * r, 0.0)) * pivot
            for l in range(j + 1, 8):
                u = cell[l][j] * r
                cols[l] = cols[l] - cols[j] * u
                for b in below:
                    b[l] = b[l] - b[j] * u
        for b, t in zip(below, range(m + 1, count)):
            total = rows[t]
            for j in range(8):
                total = total - wide(b[j] * inverse[j]) * pivots[j]
            rows[t] = total
        rows[m] = group * wide(lax.rsqrt(diagonal))
    return rows


def factor_kernel(size, parts, count_ref, place_ref, *refs):
    gram_refs = refs[:parts]
    out_ref, work, inv, left, right = refs[parts:]
    steps = size // WIDTH
    share = size // parts
    for c in range(parts):
        for t in range(c * share, size, 128):
            work[t : t + 128, c * share : (c + 1) * share] = gram_refs[c][t - c * share : t - c * share + 128, :]
    eye = (
        lax.broadcasted_iota(jnp.int32, (128, 128), 0) == lax.broadcasted_iota(jnp.int32, (128, 128), 1)
    ).astype(f32)
    trace = jnp.zeros((128, 128), f32)
    for t in range(0, size, 128):
        trace = trace + work[t : t + 128, t : t + 128] * eye
    damping = damp_share / size * jnp.sum(trace)
    for t in range(0, size, 128):
        work[t : t + 128, t : t + 128] += eye * damping

    def step(k, carry):
        start = pl.multiple_of(k * WIDTH, WIDTH)
        rows = [
            jnp.concatenate([work[pl.ds(start + t, 8), pl.ds(start, WIDTH)], eye[t : t + 8]], 1)
            for t in range(0, WIDTH, 8)
        ]
        for t, row in enumerate(eliminate(rows)):
            inv[8 * t : 8 * t + 8, :] = row[:, WIDTH:]
        inverse_terms = right_terms(inv[...])
        for k_here in range(steps):

            @pl.when(k == k_here)
            def _(k_here=k_here):
                first = k_here * WIDTH
                below = first + WIDTH
                panel = dot_nt(left_terms(work[first:, first:below]), inverse_terms)
                work[first:, first:below] = panel
                if below < size:
                    left[below:, :] = left_terms(panel[WIDTH:])
                    right[below:, :] = right_terms(panel[WIDTH:])
                col = below
                while col < size:
                    wide = 256 if col % 256 == 0 else 128
                    work[col:, col : col + wide] -= dot_nt(left[col:, :], right[col : col + wide, :])
                    col += wide

        return carry

    lax.fori_loop(0, steps, step, 0)
    scale = jnp.sqrt(2.0 / count_ref[0])
    base = pl.multiple_of(place_ref[0] * share, share)
    for t in range(0, share, 64):
        row_index = base + t + lax.broadcasted_iota(jnp.int32, (64, size), 0)
        col_index = lax.broadcasted_iota(jnp.int32, (64, size), 1)
        out_ref[t : t + 64, :] = jnp.where(row_index >= col_index, work[pl.ds(base + t, 64), :] * scale, 0.0)


def factor(grams, count, place):
    size = grams[0].shape[0]
    parts = len(grams)
    scalar = pl.BlockSpec(memory_space=pltpu.SMEM)
    whole = pl.BlockSpec(memory_space=pltpu.VMEM)
    return pl.pallas_call(
        functools.partial(factor_kernel, size, parts),
        out_shape=jax.ShapeDtypeStruct((size // parts, size), f32),
        in_specs=[scalar, scalar] + [whole] * parts,
        out_specs=whole,
        scratch_shapes=[
            pltpu.VMEM((size, size), f32),
            pltpu.VMEM((WIDTH, WIDTH), f32),
            pltpu.VMEM((size, 6 * WIDTH), bf16),
            pltpu.VMEM((size, 6 * WIDTH), bf16),
        ],
        compiler_params=pltpu.CompilerParams(vmem_limit_bytes=56 * 2**20),
        name="factor",
    )(count, place, *grams)


def shards(hidden, expert_ids):
    tokens_here, top_k, features = hidden.shape
    owners = lax.axis_size("expert")
    capacity = 3 * tokens_here * top_k // (2 * EXP_DEV * owners)
    flat_ids = expert_ids.reshape(-1)
    owner_of = flat_ids // EXP_DEV
    in_flight = flat_ids % EXP_DEV == 0
    owner_range = jnp.arange(owners, dtype=jnp.int32)
    chosen = ((owner_of[:, None] == owner_range[None, :]) & in_flight[:, None]).astype(jnp.int32)
    counts = lax.psum(jnp.sum(chosen, axis=0).astype(f32), ("dp", "expert"))
    slot_rank = jnp.sum(jnp.cumsum(chosen, axis=0) * chosen, axis=1) - 1
    target = jnp.where(in_flight, owner_of * capacity + slot_rank, owners * capacity)
    outgoing = jnp.zeros((owners * capacity, features), bf16)
    outgoing = outgoing.at[target].set(hidden.reshape(-1, features), mode="drop")
    arrived = lax.all_to_all(
        outgoing.reshape(owners, capacity, features), "expert", split_axis=0, concat_axis=0, tiled=True
    )
    received = arrived.reshape(-1, features)
    parts = lax.axis_size("dp")
    share = features // parts
    place = lax.axis_index("dp")
    core = place % 2
    grams = []
    for c in range(parts):
        gram = lax.dot_general(
            received[:, c * share :],
            received[:, c * share : (c + 1) * share],
            (((0,), (0,)), ((), ())),
            preferred_element_type=f32,
        )
        half = gram.shape[0] // 2
        mine = lax.dynamic_slice_in_dim(gram, core * half, half, 0)
        other = lax.dynamic_slice_in_dim(gram, (1 - core) * half, half, 0)
        mine = mine + lax.ppermute(other, "dp", [(i, i ^ 1) for i in range(parts)])
        mine = mine + lax.ppermute(mine, "dp", [(i, i ^ 2) for i in range(parts)])
        other = lax.ppermute(mine, "dp", [(i, i ^ 1) for i in range(parts)])
        first = jnp.where(core == 0, mine, other)
        second = jnp.where(core == 0, other, mine)
        grams.append(jnp.concatenate([first, second], 0))
    count = lax.dynamic_slice_in_dim(counts, lax.axis_index("expert"), 1, 0)
    return factor(grams, count, place[None].astype(jnp.int32))[None]


def solution(mesh):
    placed = (P(("dp", "expert"), None, None), P(("dp", "expert"), None))
    return jax.shard_map(
        shards, mesh=mesh, in_specs=placed, out_specs=P("expert", "dp", None), check_vma=False
    )
```

```python
import functools

import jax
import jax.numpy as jnp
from jax import lax
from jax.experimental import pallas as pl
from jax.experimental.pallas import tpu as pltpu
from jax.sharding import PartitionSpec as P

EXP_DEV = 4
WIDTH = 128
SECTIONS = (3, 4, 3, 2)
damp_share = 0.01
f32 = jnp.float32
bf16 = jnp.bfloat16
VMEM = pl.BlockSpec(memory_space=pltpu.VMEM)
SMEM = pl.BlockSpec(memory_space=pltpu.SMEM)
LIMIT = pltpu.CompilerParams(vmem_limit_bytes=56 * 2**20)


def split(x):
    high = x.astype(bf16)
    rest = x - high.astype(f32)
    middle = rest.astype(bf16)
    return high, middle, (rest - middle.astype(f32)).astype(bf16)


def left_terms(x, axis=1):
    h, m, l = split(x)
    return jnp.concatenate([h, h, m, m, h, l], axis)


def right_terms(x, axis=1):
    h, m, l = split(x)
    return jnp.concatenate([h, m, h, m, l, h], axis)


def dot(a, b, contract):
    return lax.dot_general(a, b, (contract, ((), ())), preferred_element_type=f32)


def dot_nt(a, b):
    return dot(left_terms(a), right_terms(b), ((1,), (1,)))


def dot_nn(a, b):
    return dot(left_terms(a), right_terms(b, 0), ((1,), (0,)))


def over_lanes(x, j):
    return jnp.broadcast_to(x[:, j : j + 1], (8, 128))


def over_rows(x, i):
    return jnp.broadcast_to(x[i : i + 1, :], x.shape)


def eliminate(rows):
    count = len(rows)
    wide = lambda v: jnp.concatenate([v, v], axis=1)
    rows = list(rows)
    sub = lax.broadcasted_iota(jnp.int32, (8, 128), 0)
    for m in range(count):
        group = rows[m]
        cols = [over_lanes(group, 8 * m + l) for l in range(8)]
        cell = [[over_rows(cols[l], i) if i >= l else None for l in range(8)] for i in range(8)]
        below = [[over_lanes(rows[t], 8 * m + l) for l in range(8)] for t in range(m + 1, count)]
        inverse, diagonal = [], None
        ratio = [[None] * 8 for _ in range(8)]
        for j in range(8):
            d = cell[j][j]
            r = pl.reciprocal(d, approx=True)
            inverse.append(r)
            diagonal = d if diagonal is None else jnp.where(sub == j, d, diagonal)
            pairs = [(i, l) for i in range(j + 1, 8) for l in range(j + 1, i + 1)]
            products = [cell[i][j] * cell[l][j] for i, l in pairs]
            for (i, l), product in zip(pairs, products):
                cell[i][l] = cell[i][l] - product * r
            for l in range(j + 1, 8):
                ratio[l][j] = cell[l][j] * r
        pivots = []
        for j in range(8):
            pivot = over_rows(group, j)
            pivots.append(pivot)
            group = group - wide(jnp.where(sub > j, cols[j] * inverse[j], 0.0)) * pivot
            for l in range(j + 1, 8):
                cols[l] = cols[l] - cols[j] * ratio[l][j]
        rows[m] = group * wide(lax.rsqrt(diagonal))
        for b, t in zip(below, range(m + 1, count)):
            for j in range(8):
                for l in range(j + 1, 8):
                    b[l] = b[l] - b[j] * ratio[l][j]
            terms = [wide(b[j] * inverse[j]) * pivots[j] for j in range(8)]
            while len(terms) > 1:
                terms = [terms[2 * i] + terms[2 * i + 1] for i in range(len(terms) // 2)]
            rows[t] = rows[t] - terms[0]
    return rows


def identity(size):
    return (
        lax.broadcasted_iota(jnp.int32, (size, size), 0) == lax.broadcasted_iota(jnp.int32, (size, size), 1)
    ).astype(f32)


def section_kernel(bounds, here, last, share, damp_ref, *refs):
    first, end = bounds[here], bounds[here + 1]
    span = end - first
    scale_ref, spot_ref, mine_ref, other_ref = refs[:4]
    lower_refs, inverse_refs = refs[4 : 4 + here], refs[4 + here : 4 + 2 * here]
    refs = refs[4 + 2 * here :]
    if last:
        out_ref, work, tile_inverse, gram_ref, lower_ref = refs
        full_inverse = None
    else:
        lower_ref, full_inverse, work, tile_inverse, gram_ref = refs
    half = span // 2
    core = spot_ref[1]
    gram_ref[pl.ds(pl.multiple_of(core * half, half), half), :] = mine_ref[...]
    gram_ref[pl.ds(pl.multiple_of((1 - core) * half, half), half), :] = other_ref[...]
    diag = gram_ref[:, first:end] + damp_ref[0] * identity(span)
    rest = [gram_ref[:, bounds[i] : bounds[i + 1]] for i in range(here)]
    for i in range(here):
        solved = dot_nt(rest[i], inverse_refs[i][...])
        lower_ref[:, bounds[i] : bounds[i + 1]] = solved
        solved_terms = left_terms(solved)
        for n in range(i + 1, here):
            other = right_terms(lower_refs[n][:, bounds[i] : bounds[i + 1]])
            rest[n] = rest[n] - dot(solved_terms, other, ((1,), (1,)))
        diag = diag - dot(solved_terms, right_terms(solved), ((1,), (1,)))
    work[...] = diag
    eye = identity(WIDTH)
    steps = span // WIDTH

    def step(k, carry):
        start = pl.multiple_of(k * WIDTH, WIDTH)
        rows = [
            jnp.concatenate([work[pl.ds(start + t, 8), pl.ds(start, WIDTH)], eye[t : t + 8]], 1)
            for t in range(0, WIDTH, 8)
        ]
        for t, row in enumerate(eliminate(rows)):
            tile_inverse[pl.ds(start + 8 * t, 8), :] = row[:, WIDTH:]
        inverse_terms = right_terms(tile_inverse[pl.ds(start, WIDTH), :])
        for k_here in range(steps):

            @pl.when(k == k_here)
            def _(k_here=k_here):
                top = k_here * WIDTH
                below = top + WIDTH
                panel = dot(left_terms(work[top:, top:below]), inverse_terms, ((1,), (1,)))
                work[top:, top:below] = panel
                if below < span:
                    work[below:, below:] -= dot(
                        left_terms(panel[WIDTH:]), right_terms(panel[WIDTH:]), ((1,), (1,))
                    )

        return carry

    lax.fori_loop(0, steps, step, 0)
    keep = lax.broadcasted_iota(jnp.int32, (span, span), 0) >= lax.broadcasted_iota(jnp.int32, (span, span), 1)
    lower = jnp.where(keep, work[...], 0.0)
    lower_ref[:, first:end] = lower
    if full_inverse is not None:
        whole = tile_inverse[:WIDTH, :]
        for k in range(1, steps):
            top = k * WIDTH
            tile = tile_inverse[top : top + WIDTH, :]
            corner = -dot_nn(tile, dot_nn(lower[top : top + WIDTH, :top], whole))
            whole = jnp.concatenate(
                [
                    jnp.concatenate([whole, jnp.zeros((top, WIDTH), f32)], 1),
                    jnp.concatenate([corner, tile], 1),
                ],
                0,
            )
        full_inverse[...] = whole
    else:
        scale = scale_ref[0]
        place = spot_ref[0]
        sources = list(lower_refs) + [lower_ref]
        for p in range(bounds[-1] // share):

            @pl.when(place == p)
            def _(p=p):
                for i, source in enumerate(sources):
                    low, high = max(bounds[i], p * share), min(bounds[i + 1], (p + 1) * share)
                    if low < high:
                        cols = bounds[i + 1]
                        out_ref[low - p * share : high - p * share, :cols] = (
                            source[low - bounds[i] : high - bounds[i], :] * scale
                        )
                        if cols < bounds[-1]:
                            out_ref[low - p * share : high - p * share, cols:] = jnp.zeros(
                                (high - low, bounds[-1] - cols), f32
                            )


def factor_section(bounds, here, share, damping, scale, spot, mine, other, lowers, inverses):
    span = bounds[here + 1] - bounds[here]
    last = here == len(bounds) - 2
    lower_shape = jax.ShapeDtypeStruct((span, bounds[here + 1]), f32)
    scratch = [
        pltpu.VMEM((span, span), f32),
        pltpu.VMEM((span, WIDTH), f32),
        pltpu.VMEM(lower_shape.shape, f32),
    ]
    if last:
        out_shape = jax.ShapeDtypeStruct((share, bounds[-1]), f32)
        scratch.append(pltpu.VMEM(lower_shape.shape, f32))
    else:
        out_shape = (lower_shape, jax.ShapeDtypeStruct((span, span), f32))
    work = 2 * 3 * (span * bounds[here] ** 2 + span**3)
    return pl.pallas_call(
        functools.partial(section_kernel, bounds, here, last, share),
        out_shape=out_shape,
        in_specs=[SMEM] * 3 + [VMEM] * (2 + 2 * here),
        out_specs=VMEM if last else (VMEM, VMEM),
        scratch_shapes=scratch,
        compiler_params=LIMIT,
        cost_estimate=pl.CostEstimate(flops=20 * work, bytes_accessed=4 * span * bounds[here + 1], transcendentals=0),
        name="factor_section",
    )(damping, scale, spot, mine, other, *lowers, *inverses)


def route_kernel(tokens, top_k, owners, capacity, ids_ref, source_ref, count_ref):
    lane = lax.broadcasted_iota(jnp.int32, (128, 128), 1)
    row = lax.broadcasted_iota(jnp.int32, (128, 128), 0)
    before = (row > lane).astype(bf16)
    carry = jnp.zeros((1, 128), f32)
    where_row = jnp.zeros((128, 128), f32)
    where_block = jnp.zeros((128, 128), f32)
    filled = jnp.zeros((128, 128), f32)
    position = row.astype(f32)
    for k in range(top_k):
        for b in range(tokens // 128):
            named = jnp.broadcast_to(ids_ref[b * 128 : (b + 1) * 128, k : k + 1], (128, 128))
            chosen = named == lane * EXP_DEV
            ones = jnp.where(chosen, 1.0, 0.0)
            ones_low = ones.astype(bf16)
            earlier = dot(before, ones_low, ((1,), (0,))) + carry
            carry = carry + jnp.sum(ones, axis=0, keepdims=True)
            rank = jnp.sum(ones * (earlier + 1.0), axis=1, keepdims=True) - 1.0
            slot = jnp.broadcast_to(rank, (128, 128)) == lane.astype(f32)
            slot_ones = jnp.where(slot, 1.0, 0.0)
            hit = dot(ones_low, slot_ones.astype(bf16), ((0,), (0,)))
            filled = filled + hit
            where_block = where_block + float(b * 128 * top_k + k) * hit
            where_row = where_row + dot(ones_low, (slot_ones * position).astype(bf16), ((0,), (0,)))
    flat = where_block + float(top_k) * where_row
    source_ref[...] = jnp.where(filled > 0.5, flat, -1.0).astype(jnp.int32)[:owners, :]
    count_ref[...] = jnp.broadcast_to(carry, (8, 128))


def route(expert_ids, owners, capacity):
    tokens, top_k = expert_ids.shape
    source, count = pl.pallas_call(
        functools.partial(route_kernel, tokens, top_k, owners, capacity),
        out_shape=(jax.ShapeDtypeStruct((owners, 128), jnp.int32), jax.ShapeDtypeStruct((8, 128), f32)),
        in_specs=[VMEM],
        out_specs=(VMEM, VMEM),
        compiler_params=LIMIT,
        name="route",
    )(expert_ids)
    return source[:, :capacity], count[0, :owners]


def swap_groups():
    groups = []
    for x_lo in range(2):
        for core in range(2):
            groups.append([(2 * (x_lo ^ (e % 2)) + core) * 32 + e for e in range(32)])
    return groups


def after(value, *others):
    return lax.optimization_barrier((value, *others))[0]


def shards(hidden, expert_ids):
    tokens_here, top_k, features = hidden.shape
    owners = lax.axis_size("expert")
    parts = lax.axis_size("dp")
    share = features // parts
    capacity = 3 * tokens_here * top_k // (2 * EXP_DEV * owners)
    bounds = [0]
    for s in SECTIONS:
        bounds.append(bounds[-1] + s * WIDTH)
    sections = len(SECTIONS)
    source, counts = route(expert_ids, owners, capacity)
    slots = source.reshape(-1)
    used = (slots >= 0)[:, None]
    taken = jnp.take(hidden.reshape(-1, features), jnp.maximum(slots, 0), axis=0, mode="clip")
    place = lax.axis_index("dp")
    core = place % 2
    spot = jnp.stack([place, core]).astype(jnp.int32)
    groups = swap_groups()
    received = jnp.zeros((owners * capacity, features), bf16)
    lowers, inverses, grams = [], [], []
    arrived = None
    for c in range(sections):
        low, high = bounds[c], bounds[c + 1]
        piece = jnp.where(used, taken[:, low:high], jnp.zeros((), bf16)).reshape(owners, capacity, -1)
        waits = [] if c == 0 else [arrived]
        if c == 1:
            waits.append(facts)
        if c >= 2:
            waits.append(grams[c - 2])
        if c >= 3:
            waits.append(lowers[c - 3])
        if waits:
            piece = after(piece, *waits)
        arrived = lax.all_to_all(
            piece, ("dp", "expert"), split_axis=0, concat_axis=0, tiled=True, axis_index_groups=groups
        )
        if c == 0:
            squares = jnp.where(used, jnp.square(taken.astype(f32)), 0.0).reshape(owners, -1)
            facts = jnp.tile(jnp.stack([counts, jnp.sum(squares, axis=1)], 1), (parts, 1))
            facts = after(facts, arrived)
            facts = lax.all_to_all(facts, ("dp", "expert"), split_axis=0, concat_axis=0, tiled=True)
            total = jnp.sum(facts, axis=0)
            scale = jnp.sqrt(2.0 / total[0])[None]
            damping = (damp_share * total[1] / features)[None]
        rows = arrived.reshape(owners * capacity, -1)
        received = received.at[:, low:high].set(rows)
        gram = lax.dot_general(rows, received[:, :high], (((0,), (0,)), ((), ())), preferred_element_type=f32)
        half = gram.shape[0] // 2
        mine = lax.dynamic_slice_in_dim(gram, core * half, half, 0)
        other = lax.dynamic_slice_in_dim(gram, (1 - core) * half, half, 0)
        grams.append(other)
        mine = mine + lax.ppermute(other, "dp", [(i, i ^ 1) for i in range(parts)])
        mine = mine + lax.ppermute(mine, "dp", [(i, i ^ 2) for i in range(parts)])
        other = lax.ppermute(mine, "dp", [(i, i ^ 1) for i in range(parts)])
        result = factor_section(bounds, c, share, damping, scale, spot, mine, other, lowers, inverses)
        if c == sections - 1:
            return result[None]
        lowers.append(result[0])
        inverses.append(result[1])


def solution(mesh):
    placed = (P(("dp", "expert"), None, None), P(("dp", "expert"), None))
    return jax.shard_map(
        shards, mesh=mesh, in_specs=placed, out_specs=P("expert", "dp", None), check_vma=False
    )
```

```python
import functools

import jax
import jax.numpy as jnp
from jax import lax
from jax.experimental import pallas as pl
from jax.experimental.pallas import tpu as pltpu
from jax.sharding import PartitionSpec as P

EXP_DEV = 4
WIDTH = 128
CHUNKS = ((4, 4), (2, 2))
HELD = (0, 1)
EARLY = {}
damp_share = 0.01
f32 = jnp.float32
bf16 = jnp.bfloat16
VMEM = pl.BlockSpec(memory_space=pltpu.VMEM)
SMEM = pl.BlockSpec(memory_space=pltpu.SMEM)
LIMIT = pltpu.CompilerParams(vmem_limit_bytes=56 * 2**20)


def split(x):
    high = x.astype(bf16)
    rest = x - high.astype(f32)
    middle = rest.astype(bf16)
    return high, middle, (rest - middle.astype(f32)).astype(bf16)


def left_terms(x, axis=1):
    h, m, l = split(x)
    return jnp.concatenate([h, h, m, m, h, l], axis)


def right_terms(x, axis=1):
    h, m, l = split(x)
    return jnp.concatenate([h, m, h, m, l, h], axis)


def dot(a, b, contract):
    return lax.dot_general(a, b, (contract, ((), ())), preferred_element_type=f32)


def dot_nt(a, b):
    return dot(left_terms(a), right_terms(b), ((1,), (1,)))


def dot_nn(a, b):
    return dot(left_terms(a), right_terms(b, 0), ((1,), (0,)))


def over_lanes(x, j):
    return jnp.broadcast_to(x[:, j : j + 1], (8, 128))


def over_rows(x, i):
    return jnp.broadcast_to(x[i : i + 1, :], x.shape)


def eliminate(rows):
    count = len(rows)
    wide = lambda v: jnp.concatenate([v, v], axis=1)
    rows = list(rows)
    sub = lax.broadcasted_iota(jnp.int32, (8, 128), 0)
    for m in range(count):
        group = rows[m]
        cols = [over_lanes(group, 8 * m + l) for l in range(8)]
        cell = [[over_rows(cols[l], i) if i >= l else None for l in range(8)] for i in range(8)]
        below = [[over_lanes(rows[t], 8 * m + l) for l in range(8)] for t in range(m + 1, count)]
        inverse, diagonal = [], None
        ratio = [[None] * 8 for _ in range(8)]
        for j in range(8):
            d = cell[j][j]
            r = pl.reciprocal(d, approx=True)
            inverse.append(r)
            diagonal = d if diagonal is None else jnp.where(sub == j, d, diagonal)
            pairs = [(i, l) for i in range(j + 1, 8) for l in range(j + 1, i + 1)]
            products = [cell[i][j] * cell[l][j] for i, l in pairs]
            for (i, l), product in zip(pairs, products):
                cell[i][l] = cell[i][l] - product * r
            for l in range(j + 1, 8):
                ratio[l][j] = cell[l][j] * r
        pivots = []
        for j in range(8):
            pivot = over_rows(group, j)
            pivots.append(pivot)
            group = group - wide(jnp.where(sub > j, cols[j] * inverse[j], 0.0)) * pivot
            for l in range(j + 1, 8):
                cols[l] = cols[l] - cols[j] * ratio[l][j]
        rows[m] = group * wide(lax.rsqrt(diagonal))
        for b, t in zip(below, range(m + 1, count)):
            for j in range(8):
                for l in range(j + 1, 8):
                    b[l] = b[l] - b[j] * ratio[l][j]
            terms = [wide(b[j] * inverse[j]) * pivots[j] for j in range(8)]
            while len(terms) > 1:
                terms = [terms[2 * i] + terms[2 * i + 1] for i in range(len(terms) // 2)]
            rows[t] = rows[t] - terms[0]
    return rows


def identity(size):
    return (
        lax.broadcasted_iota(jnp.int32, (size, size), 0) == lax.broadcasted_iota(jnp.int32, (size, size), 1)
    ).astype(f32)


def section_kernel(bounds, here, last, share, damp_ref, *refs):
    first, end = bounds[here], bounds[here + 1]
    span = end - first
    scale_ref, spot_ref, mine_ref, other_ref = refs[:4]
    lower_refs, inverse_refs = refs[4 : 4 + here], refs[4 + here : 4 + 2 * here]
    refs = refs[4 + 2 * here :]
    if last:
        out_ref, work, tile_inverse, gram_ref, lower_ref = refs
        full_inverse = None
    else:
        lower_ref, full_inverse, work, tile_inverse, gram_ref = refs
    half = span // 2
    core = spot_ref[1]
    gram_ref[pl.ds(pl.multiple_of(core * half, half), half), :] = mine_ref[...]
    gram_ref[pl.ds(pl.multiple_of((1 - core) * half, half), half), :] = other_ref[...]
    diag = gram_ref[:, first:end] + damp_ref[0] * identity(span)
    rest = [gram_ref[:, bounds[i] : bounds[i + 1]] for i in range(here)]
    for i in range(here):
        solved = dot_nt(rest[i], inverse_refs[i][...])
        lower_ref[:, bounds[i] : bounds[i + 1]] = solved
        solved_terms = left_terms(solved)
        for n in range(i + 1, here):
            other = right_terms(lower_refs[n][:, bounds[i] : bounds[i + 1]])
            rest[n] = rest[n] - dot(solved_terms, other, ((1,), (1,)))
        diag = diag - dot(solved_terms, right_terms(solved), ((1,), (1,)))
    work[...] = diag
    eye = identity(WIDTH)
    steps = span // WIDTH

    def step(k, carry):
        start = pl.multiple_of(k * WIDTH, WIDTH)
        rows = [
            jnp.concatenate([work[pl.ds(start + t, 8), pl.ds(start, WIDTH)], eye[t : t + 8]], 1)
            for t in range(0, WIDTH, 8)
        ]
        for t, row in enumerate(eliminate(rows)):
            tile_inverse[pl.ds(start + 8 * t, 8), :] = row[:, WIDTH:]
        inverse_terms = right_terms(tile_inverse[pl.ds(start, WIDTH), :])
        for k_here in range(steps):

            @pl.when(k == k_here)
            def _(k_here=k_here):
                top = k_here * WIDTH
                below = top + WIDTH
                panel = dot(left_terms(work[top:, top:below]), inverse_terms, ((1,), (1,)))
                work[top:, top:below] = panel
                if below < span:
                    work[below:, below:] -= dot(
                        left_terms(panel[WIDTH:]), right_terms(panel[WIDTH:]), ((1,), (1,))
                    )

        return carry

    lax.fori_loop(0, steps, step, 0)
    keep = lax.broadcasted_iota(jnp.int32, (span, span), 0) >= lax.broadcasted_iota(jnp.int32, (span, span), 1)
    lower = jnp.where(keep, work[...], 0.0)
    lower_ref[:, first:end] = lower
    if full_inverse is not None:
        whole = tile_inverse[:WIDTH, :]
        for k in range(1, steps):
            top = k * WIDTH
            tile = tile_inverse[top : top + WIDTH, :]
            corner = -dot_nn(tile, dot_nn(lower[top : top + WIDTH, :top], whole))
            whole = jnp.concatenate(
                [
                    jnp.concatenate([whole, jnp.zeros((top, WIDTH), f32)], 1),
                    jnp.concatenate([corner, tile], 1),
                ],
                0,
            )
        full_inverse[...] = whole
    else:
        scale = scale_ref[0]
        place = spot_ref[0]
        sources = list(lower_refs) + [lower_ref]
        for p in range(bounds[-1] // share):

            @pl.when(place == p)
            def _(p=p):
                for i, source in enumerate(sources):
                    low, high = max(bounds[i], p * share), min(bounds[i + 1], (p + 1) * share)
                    if low < high:
                        cols = bounds[i + 1]
                        out_ref[low - p * share : high - p * share, :cols] = (
                            source[low - bounds[i] : high - bounds[i], :] * scale
                        )
                        if cols < bounds[-1]:
                            out_ref[low - p * share : high - p * share, cols:] = jnp.zeros(
                                (high - low, bounds[-1] - cols), f32
                            )


def factor_section(bounds, here, share, damping, scale, spot, mine, other, lowers, inverses):
    span = bounds[here + 1] - bounds[here]
    last = here == len(bounds) - 2
    lower_shape = jax.ShapeDtypeStruct((span, bounds[here + 1]), f32)
    scratch = [
        pltpu.VMEM((span, span), f32),
        pltpu.VMEM((span, WIDTH), f32),
        pltpu.VMEM(lower_shape.shape, f32),
    ]
    if last:
        out_shape = jax.ShapeDtypeStruct((share, bounds[-1]), f32)
        scratch.append(pltpu.VMEM(lower_shape.shape, f32))
    else:
        out_shape = (lower_shape, jax.ShapeDtypeStruct((span, span), f32))
    return pl.pallas_call(
        functools.partial(section_kernel, bounds, here, last, share),
        out_shape=out_shape,
        in_specs=[SMEM] * 3 + [VMEM] * (2 + 2 * here),
        out_specs=VMEM if last else (VMEM, VMEM),
        scratch_shapes=scratch,
        compiler_params=LIMIT,
        cost_estimate=pl.CostEstimate(flops=WIDTH * span, bytes_accessed=span, transcendentals=0),
        name="factor_section",
    )(damping, scale, spot, mine, other, *lowers, *inverses)


def route_kernel(tokens, top_k, owners, capacity, ids_ref, source_ref, count_ref):
    blocks = tokens // 128
    owner = lax.broadcasted_iota(jnp.int32, (owners, 128), 0) * EXP_DEV
    position = lax.broadcasted_iota(jnp.int32, (owners, 128), 1).astype(f32)
    slot = lax.broadcasted_iota(jnp.int32, (capacity, 128), 0).astype(f32)
    row = lax.broadcasted_iota(jnp.int32, (128, 256), 0)
    col = lax.broadcasted_iota(jnp.int32, (128, 256), 1)
    earlier_and_all = jnp.where((row < col) | (col >= 128), 1.0, 0.0).astype(bf16)
    carry = jnp.zeros((owners, 128), f32)
    found = jnp.zeros((3 * owners, capacity), f32)
    for k in range(top_k):
        chosen = [
            jnp.where(
                jnp.broadcast_to(ids_ref[k : k + 1, b * 128 : (b + 1) * 128], (owners, 128)) == owner, 1.0, 0.0
            )
            for b in range(blocks)
        ]
        sums = dot(jnp.concatenate(chosen, 0).astype(bf16), earlier_and_all, ((1,), (0,)))
        marks, slots = [], []
        for b in range(blocks):
            ones = chosen[b]
            part = sums[b * owners : (b + 1) * owners]
            rank = jnp.sum(ones * (part[:, :128] + carry), axis=0, keepdims=True)
            carry = carry + part[:, 128:]
            marks.append(jnp.concatenate([ones, ones * position, ones * float(b * top_k + k)], 0).astype(bf16))
            slots.append(jnp.where(jnp.broadcast_to(rank, (capacity, 128)) == slot, 1.0, 0.0).astype(bf16))
        found = found + dot(jnp.concatenate(marks, 1), jnp.concatenate(slots, 1), ((1,), (1,)))
    filled = found[:owners] > 0.5
    place = found[owners : 2 * owners].astype(jnp.int32)
    block = found[2 * owners :].astype(jnp.int32)
    flat = (block // top_k) * (128 * top_k) + block % top_k + place * top_k
    source_ref[...] = jnp.where(filled, flat, -1)
    count_ref[...] = carry


def route(expert_ids, owners, capacity):
    tokens, top_k = expert_ids.shape
    source, count = pl.pallas_call(
        functools.partial(route_kernel, tokens, top_k, owners, capacity),
        out_shape=(jax.ShapeDtypeStruct((owners, capacity), jnp.int32), jax.ShapeDtypeStruct((owners, 128), f32)),
        in_specs=[VMEM],
        out_specs=(VMEM, VMEM),
        compiler_params=LIMIT,
        name="route",
    )(expert_ids.T)
    return source, count[:, 0]


def swap_groups():
    groups = []
    for x_lo in range(2):
        for core in range(2):
            groups.append([(2 * (x_lo ^ (e % 2)) + core) * 32 + e for e in range(32)])
    return groups


def after(value, *others):
    return lax.optimization_barrier((value, *others))[0]


def summed_over_all(value):
    for axis in ("dp", "expert"):
        size = lax.axis_size(axis)
        step = 1
        while step < size:
            value = value + lax.ppermute(value, axis, [(i, i ^ step) for i in range(size)])
            step *= 2
    return value


def shards(hidden, expert_ids):
    tokens_here, top_k, features = hidden.shape
    owners = lax.axis_size("expert")
    parts = lax.axis_size("dp")
    share = features // parts
    capacity = 3 * tokens_here * top_k // (2 * EXP_DEV * owners)
    bounds = [0]
    for sections in CHUNKS:
        for s in sections:
            bounds.append(bounds[-1] + s * WIDTH)
    source, counts = route(expert_ids, owners, capacity)
    slots = source.reshape(-1)
    used = (slots >= 0)[:, None]
    taken = hidden.reshape(-1, features).at[jnp.maximum(slots, 0)].get(mode="promise_in_bounds")
    place = lax.axis_index("dp")
    core = place % 2
    spot = jnp.stack([place, core]).astype(jnp.int32)
    groups = swap_groups()

    pieces, low = [], 0
    for sections in CHUNKS:
        high = low + WIDTH * sum(sections)
        pieces.append(jnp.where(used, taken[:, low:high], jnp.zeros((), bf16)).reshape(owners, capacity, -1))
        low = high
    def send(piece):
        return lax.all_to_all(
            piece, ("dp", "expert"), split_axis=0, concat_axis=0, tiled=True, axis_index_groups=groups
        )

    received, half_sums, pair_sums, lowers, inverses = [], [], {}, [], []

    def sum_grams(rows, sections):
        earlier = list(received)
        received.append(rows)
        first = sum(r.shape[1] for r in earlier)
        other = None
        for _ in sections:
            c = len(half_sums)
            if other is not None:
                rows = after(rows, other)
            low, high = bounds[c] - first, bounds[c + 1] - first
            gram = [
                lax.dot_general(
                    rows[:, low:high], against, (((0,), (0,)), ((), ())), preferred_element_type=f32
                )
                for against in earlier + [rows[:, :high]]
            ]
            gram = jnp.concatenate(gram, 1)
            half = gram.shape[0] // 2
            mine = lax.dynamic_slice_in_dim(gram, core * half, half, 0)
            other = lax.dynamic_slice_in_dim(gram, (1 - core) * half, half, 0)
            half_sums.append(mine + lax.ppermute(other, "dp", [(i, i ^ 1) for i in range(parts)]))

    def pair_sum(c):
        if c not in pair_sums:
            swapped = lax.ppermute(half_sums[c], "dp", [(i, i ^ 2) for i in range(parts)])
            pair_sums[c] = half_sums[c] + after(swapped, *lowers[-1:])
        return pair_sums[c]

    def factor(c):
        mine = pair_sum(c)
        other = lax.ppermute(mine, "dp", [(i, i ^ 1) for i in range(parts)])
        early = [pair_sum(i) for i in EARLY.get(c, ())]
        mine = after(mine, *half_sums[c + 1 :], *early)
        result = factor_section(bounds, c, share, damping, scale, spot, mine, other, lowers, inverses)
        if c < len(bounds) - 2:
            lowers.append(result[0])
            inverses.append(result[1])
        return result

    sent = send(pieces[0])
    squares = jnp.where(used, jnp.square(taken.astype(f32)), 0.0).reshape(owners, -1)
    facts = summed_over_all(jnp.stack([counts, jnp.sum(squares, axis=1)], 1))
    total = lax.dynamic_slice_in_dim(facts, lax.axis_index("expert"), 1, 0)[0]
    scale = jnp.sqrt(2.0 / total[0])[None]
    damping = (damp_share * total[1] / features)[None]
    sum_grams(after(sent, facts).reshape(owners * capacity, -1), CHUNKS[0])
    for chunk in range(1, len(CHUNKS)):
        sent = send(after(pieces[chunk], sent))
        done = len(half_sums) - HELD[chunk]
        while len(lowers) < done:
            factor(len(lowers))
        rows = after(sent, lowers[-1]) if lowers else sent
        sum_grams(rows.reshape(owners * capacity, -1), CHUNKS[chunk])
    while len(lowers) < len(half_sums) - 1:
        factor(len(lowers))
    return factor(len(lowers))[None]


def solution(mesh):
    placed = (P(("dp", "expert"), None, None), P(("dp", "expert"), None))
    return jax.shard_map(
        shards, mesh=mesh, in_specs=placed, out_specs=P("expert", "dp", None), check_vma=False
    )
```

```python
import functools

import jax
import jax.numpy as jnp
from jax import lax
from jax.experimental import pallas as pl
from jax.experimental.pallas import tpu as pltpu
from jax.sharding import PartitionSpec as P

EXP_DEV = 4
WIDTH = 128
CHUNKS = ((2, 4), (2, 2, 2))
HELD = (0, 0)
damp_share = 0.01
f32 = jnp.float32
bf16 = jnp.bfloat16
VMEM = pl.BlockSpec(memory_space=pltpu.VMEM)
SMEM = pl.BlockSpec(memory_space=pltpu.SMEM)
LIMIT = pltpu.CompilerParams(vmem_limit_bytes=56 * 2**20)


def split(x):
    high = x.astype(bf16)
    rest = x - high.astype(f32)
    middle = rest.astype(bf16)
    return high, middle, (rest - middle.astype(f32)).astype(bf16)


def left_terms(x, axis=1):
    h, m, l = split(x)
    return jnp.concatenate([h, h, m, m, h, l], axis)


def right_terms(x, axis=1):
    h, m, l = split(x)
    return jnp.concatenate([h, m, h, m, l, h], axis)


def dot(a, b, contract):
    return lax.dot_general(a, b, (contract, ((), ())), preferred_element_type=f32)


def dot_nt(a, b):
    return dot(left_terms(a), right_terms(b), ((1,), (1,)))


def dot_nn(a, b):
    return dot(left_terms(a), right_terms(b, 0), ((1,), (0,)))


def over_lanes(x, j):
    return jnp.broadcast_to(x[:, j : j + 1], (8, 128))


def over_rows(x, i):
    return jnp.broadcast_to(x[i : i + 1, :], x.shape)


def eliminate(rows):
    count = len(rows)
    wide = lambda v: jnp.concatenate([v, v], axis=1)
    rows = list(rows)
    sub = lax.broadcasted_iota(jnp.int32, (8, 128), 0)
    for m in range(count):
        group = rows[m]
        cols = [over_lanes(group, 8 * m + l) for l in range(8)]
        cell = [[over_rows(cols[l], i) if i >= l else None for l in range(8)] for i in range(8)]
        below = [[over_lanes(rows[t], 8 * m + l) for l in range(8)] for t in range(m + 1, count)]
        inverse, diagonal = [], None
        ratio = [[None] * 8 for _ in range(8)]
        for j in range(8):
            d = cell[j][j]
            r = pl.reciprocal(d, approx=True)
            inverse.append(r)
            diagonal = d if diagonal is None else jnp.where(sub == j, d, diagonal)
            pairs = [(i, l) for i in range(j + 1, 8) for l in range(j + 1, i + 1)]
            products = [cell[i][j] * cell[l][j] for i, l in pairs]
            for (i, l), product in zip(pairs, products):
                cell[i][l] = cell[i][l] - product * r
            for l in range(j + 1, 8):
                ratio[l][j] = cell[l][j] * r
        pivots = []
        for j in range(8):
            pivot = over_rows(group, j)
            pivots.append(pivot)
            group = group - wide(jnp.where(sub > j, cols[j] * inverse[j], 0.0)) * pivot
            for l in range(j + 1, 8):
                cols[l] = cols[l] - cols[j] * ratio[l][j]
        rows[m] = group * wide(lax.rsqrt(diagonal))
        for b, t in zip(below, range(m + 1, count)):
            for j in range(8):
                for l in range(j + 1, 8):
                    b[l] = b[l] - b[j] * ratio[l][j]
            terms = [wide(b[j] * inverse[j]) * pivots[j] for j in range(8)]
            while len(terms) > 1:
                terms = [terms[2 * i] + terms[2 * i + 1] for i in range(len(terms) // 2)]
            rows[t] = rows[t] - terms[0]
    return rows


def identity(size):
    return (
        lax.broadcasted_iota(jnp.int32, (size, size), 0) == lax.broadcasted_iota(jnp.int32, (size, size), 1)
    ).astype(f32)


def section_kernel(bounds, here, last, share, damp_ref, *refs):
    first, end = bounds[here], bounds[here + 1]
    span = end - first
    scale_ref, spot_ref, mine_ref, other_ref = refs[:4]
    lower_refs, inverse_refs = refs[4 : 4 + here], refs[4 + here : 4 + 2 * here]
    refs = refs[4 + 2 * here :]
    if last:
        out_ref, work, tile_inverse, gram_ref, lower_ref = refs
        full_inverse = None
    else:
        lower_ref, full_inverse, work, tile_inverse, gram_ref = refs
    half = span // 2
    core = spot_ref[1]
    gram_ref[pl.ds(pl.multiple_of(core * half, half), half), :] = mine_ref[...]
    gram_ref[pl.ds(pl.multiple_of((1 - core) * half, half), half), :] = other_ref[...]
    diag = gram_ref[:, first:end] + damp_ref[0] * identity(span)
    rest = [gram_ref[:, bounds[i] : bounds[i + 1]] for i in range(here)]
    for i in range(here):
        solved = dot_nt(rest[i], inverse_refs[i][...])
        lower_ref[:, bounds[i] : bounds[i + 1]] = solved
        solved_terms = left_terms(solved)
        for n in range(i + 1, here):
            other = right_terms(lower_refs[n][:, bounds[i] : bounds[i + 1]])
            rest[n] = rest[n] - dot(solved_terms, other, ((1,), (1,)))
        diag = diag - dot(solved_terms, right_terms(solved), ((1,), (1,)))
    work[...] = diag
    eye = identity(WIDTH)
    steps = span // WIDTH

    def step(k, carry):
        start = pl.multiple_of(k * WIDTH, WIDTH)
        rows = [
            jnp.concatenate([work[pl.ds(start + t, 8), pl.ds(start, WIDTH)], eye[t : t + 8]], 1)
            for t in range(0, WIDTH, 8)
        ]
        for t, row in enumerate(eliminate(rows)):
            tile_inverse[pl.ds(start + 8 * t, 8), :] = row[:, WIDTH:]
        inverse_terms = right_terms(tile_inverse[pl.ds(start, WIDTH), :])
        for k_here in range(steps):

            @pl.when(k == k_here)
            def _(k_here=k_here):
                top = k_here * WIDTH
                below = top + WIDTH
                panel = dot(left_terms(work[top:, top:below]), inverse_terms, ((1,), (1,)))
                work[top:, top:below] = panel
                if below < span:
                    work[below:, below:] -= dot(
                        left_terms(panel[WIDTH:]), right_terms(panel[WIDTH:]), ((1,), (1,))
                    )

        return carry

    lax.fori_loop(0, steps, step, 0)
    keep = lax.broadcasted_iota(jnp.int32, (span, span), 0) >= lax.broadcasted_iota(jnp.int32, (span, span), 1)
    lower = jnp.where(keep, work[...], 0.0)
    lower_ref[:, first:end] = lower
    if full_inverse is not None:
        whole = tile_inverse[:WIDTH, :]
        for k in range(1, steps):
            top = k * WIDTH
            tile = tile_inverse[top : top + WIDTH, :]
            corner = -dot_nn(tile, dot_nn(lower[top : top + WIDTH, :top], whole))
            whole = jnp.concatenate(
                [
                    jnp.concatenate([whole, jnp.zeros((top, WIDTH), f32)], 1),
                    jnp.concatenate([corner, tile], 1),
                ],
                0,
            )
        full_inverse[...] = whole
    else:
        scale = scale_ref[0]
        place = spot_ref[0]
        sources = list(lower_refs) + [lower_ref]
        for p in range(bounds[-1] // share):

            @pl.when(place == p)
            def _(p=p):
                for i, source in enumerate(sources):
                    low, high = max(bounds[i], p * share), min(bounds[i + 1], (p + 1) * share)
                    if low < high:
                        cols = bounds[i + 1]
                        out_ref[low - p * share : high - p * share, :cols] = (
                            source[low - bounds[i] : high - bounds[i], :] * scale
                        )
                        if cols < bounds[-1]:
                            out_ref[low - p * share : high - p * share, cols:] = jnp.zeros(
                                (high - low, bounds[-1] - cols), f32
                            )


def factor_section(bounds, here, share, damping, scale, spot, mine, other, lowers, inverses):
    span = bounds[here + 1] - bounds[here]
    last = here == len(bounds) - 2
    lower_shape = jax.ShapeDtypeStruct((span, bounds[here + 1]), f32)
    scratch = [
        pltpu.VMEM((span, span), f32),
        pltpu.VMEM((span, WIDTH), f32),
        pltpu.VMEM(lower_shape.shape, f32),
    ]
    if last:
        out_shape = jax.ShapeDtypeStruct((share, bounds[-1]), f32)
        scratch.append(pltpu.VMEM(lower_shape.shape, f32))
    else:
        out_shape = (lower_shape, jax.ShapeDtypeStruct((span, span), f32))
    return pl.pallas_call(
        functools.partial(section_kernel, bounds, here, last, share),
        out_shape=out_shape,
        in_specs=[SMEM] * 3 + [VMEM] * (2 + 2 * here),
        out_specs=VMEM if last else (VMEM, VMEM),
        scratch_shapes=scratch,
        compiler_params=LIMIT,
        cost_estimate=pl.CostEstimate(flops=WIDTH * span, bytes_accessed=span, transcendentals=0),
        name="factor_section",
    )(damping, scale, spot, mine, other, *lowers, *inverses)


def route_kernel(tokens, top_k, owners, capacity, ids_ref, source_ref, count_ref):
    blocks = tokens // 128
    owner = lax.broadcasted_iota(jnp.int32, (owners, 128), 0) * EXP_DEV
    position = lax.broadcasted_iota(jnp.int32, (owners, 128), 1).astype(f32)
    slot = lax.broadcasted_iota(jnp.int32, (capacity, 128), 0).astype(f32)
    row = lax.broadcasted_iota(jnp.int32, (128, 256), 0)
    col = lax.broadcasted_iota(jnp.int32, (128, 256), 1)
    earlier_and_all = jnp.where((row < col) | (col >= 128), 1.0, 0.0).astype(bf16)
    carry = jnp.zeros((owners, 128), f32)
    found = jnp.zeros((3 * owners, capacity), f32)
    for k in range(top_k):
        chosen = [
            jnp.where(
                jnp.broadcast_to(ids_ref[k : k + 1, b * 128 : (b + 1) * 128], (owners, 128)) == owner, 1.0, 0.0
            )
            for b in range(blocks)
        ]
        sums = dot(jnp.concatenate(chosen, 0).astype(bf16), earlier_and_all, ((1,), (0,)))
        marks, slots = [], []
        for b in range(blocks):
            ones = chosen[b]
            part = sums[b * owners : (b + 1) * owners]
            rank = jnp.sum(ones * (part[:, :128] + carry), axis=0, keepdims=True)
            carry = carry + part[:, 128:]
            marks.append(jnp.concatenate([ones, ones * position, ones * float(b * top_k + k)], 0).astype(bf16))
            slots.append(jnp.where(jnp.broadcast_to(rank, (capacity, 128)) == slot, 1.0, 0.0).astype(bf16))
        found = found + dot(jnp.concatenate(marks, 1), jnp.concatenate(slots, 1), ((1,), (1,)))
    filled = found[:owners] > 0.5
    place = found[owners : 2 * owners].astype(jnp.int32)
    block = found[2 * owners :].astype(jnp.int32)
    flat = (block // top_k) * (128 * top_k) + block % top_k + place * top_k
    source_ref[...] = jnp.where(filled, flat, -1)
    count_ref[...] = carry


def route(expert_ids, owners, capacity):
    tokens, top_k = expert_ids.shape
    source, count = pl.pallas_call(
        functools.partial(route_kernel, tokens, top_k, owners, capacity),
        out_shape=(jax.ShapeDtypeStruct((owners, capacity), jnp.int32), jax.ShapeDtypeStruct((owners, 128), f32)),
        in_specs=[VMEM],
        out_specs=(VMEM, VMEM),
        compiler_params=LIMIT,
        name="route",
    )(expert_ids.T)
    return source, count[:, 0]


def swap_groups():
    groups = []
    for x_lo in range(2):
        for core in range(2):
            groups.append([(2 * (x_lo ^ (e % 2)) + core) * 32 + e for e in range(32)])
    return groups


def after(value, *others):
    return lax.optimization_barrier((value, *others))[0]


def summed_over_all(value):
    for axis, masks in (("dp", (1, 2, 3)), ("expert", (1, 2, 3)), ("expert", (4, 8, 12)), ("expert", (16,))):
        pairs = range(lax.axis_size(axis))
        value = value + sum(lax.ppermute(value, axis, [(i, i ^ mask) for i in pairs]) for mask in masks)
    return value


def shards(hidden, expert_ids):
    tokens_here, top_k, features = hidden.shape
    owners = lax.axis_size("expert")
    parts = lax.axis_size("dp")
    share = features // parts
    capacity = 3 * tokens_here * top_k // (2 * EXP_DEV * owners)
    bounds = [0]
    for sections in CHUNKS:
        for s in sections:
            bounds.append(bounds[-1] + s * WIDTH)
    source, counts = route(expert_ids, owners, capacity)
    slots = source.reshape(-1)
    used = (slots >= 0)[:, None]
    taken = hidden.reshape(-1, features).at[jnp.maximum(slots, 0)].get(mode="promise_in_bounds")
    place = lax.axis_index("dp")
    core = place % 2
    spot = jnp.stack([place, core]).astype(jnp.int32)
    groups = swap_groups()

    pieces, low = [], 0
    for sections in CHUNKS:
        high = low + WIDTH * sum(sections)
        pieces.append(jnp.where(used, taken[:, low:high], jnp.zeros((), bf16)).reshape(owners, capacity, -1))
        low = high
    def send(piece):
        return lax.all_to_all(
            piece, ("dp", "expert"), split_axis=0, concat_axis=0, tiled=True, axis_index_groups=groups
        )

    received, half_sums, swaps, lowers, inverses = [], [], [], [], []

    def sum_grams(rows, sections, whole):
        earlier = list(received)
        received.append(rows)
        first = sum(r.shape[1] for r in earlier)

        def gram_of(low, high):
            parts_here = [
                lax.dot_general(
                    rows[:, low:high], against, (((0,), (0,)), ((), ())), preferred_element_type=f32
                )
                for against in earlier + [rows[:, :high]]
            ]
            return jnp.concatenate(parts_here, 1) if earlier else parts_here[0]

        everything = gram_of(0, rows.shape[1]) if whole else None
        other = None
        for _ in sections:
            c = len(half_sums)
            low, high = bounds[c] - first, bounds[c + 1] - first
            if other is not None and not whole:
                rows = after(rows, other)
            gram = everything[low:high, : bounds[c + 1]] if whole else gram_of(low, high)
            half = gram.shape[0] // 2
            mine = lax.dynamic_slice_in_dim(gram, core * half, half, 0)
            other = lax.dynamic_slice_in_dim(gram, (1 - core) * half, half, 0)
            half_sums.append(mine + lax.ppermute(other, "dp", [(i, i ^ 1) for i in range(parts)]))

    def swap_halves():
        while len(swaps) < len(half_sums):
            half_sum = half_sums[len(swaps)]
            if len(swaps) == 1:
                half_sum = after(half_sum, swaps[0])
            swaps.append(lax.ppermute(half_sum, "dp", [(i, i ^ 2) for i in range(parts)]))

    def factor(c):
        mine = half_sums[c] + after(swaps[c], *lowers[-1:])
        other = lax.ppermute(mine, "dp", [(i, i ^ 1) for i in range(parts)])
        mine = after(mine, *half_sums[c + 1 :])
        result = factor_section(bounds, c, share, damping, scale, spot, mine, other, lowers, inverses)
        if c < len(bounds) - 2:
            lowers.append(result[0])
            inverses.append(result[1])
        return result

    sent = send(pieces[0])
    squares = jnp.where(used, jnp.square(taken.astype(f32)), 0.0).reshape(owners, -1)
    facts = jnp.stack([counts, jnp.sum(squares, axis=1)], 1)
    sent = after(sent, facts, pieces[1])
    facts = summed_over_all(after(facts, sent))
    total = lax.dynamic_slice_in_dim(facts, lax.axis_index("expert"), 1, 0)[0]
    scale = jnp.sqrt(2.0 / total[0])[None]
    damping = (damp_share * total[1] / features)[None]
    sum_grams(sent.reshape(owners * capacity, -1), CHUNKS[0], False)
    swap_halves()
    pieces[1] = after(pieces[1], facts, *half_sums)
    for chunk in range(1, len(CHUNKS)):
        sent = send(after(pieces[chunk], sent))
        done = len(half_sums) - HELD[chunk]
        while len(lowers) < done:
            factor(len(lowers))
        rows = after(sent, lowers[-1]) if lowers else sent
        sum_grams(rows.reshape(owners * capacity, -1), CHUNKS[chunk], True)
        swap_halves()
    while len(lowers) < len(half_sums) - 1:
        factor(len(lowers))
    return factor(len(lowers))[None]


def solution(mesh):
    placed = (P(("dp", "expert"), None, None), P(("dp", "expert"), None))
    return jax.shard_map(
        shards, mesh=mesh, in_specs=placed, out_specs=P("expert", "dp", None), check_vma=False
    )
```

```python
import functools

import jax
import jax.numpy as jnp
from jax import lax
from jax.experimental import pallas as pl
from jax.experimental.pallas import tpu as pltpu
from jax.sharding import PartitionSpec as P

EXP_DEV = 4
WIDTH = 128
CHUNKS = ((3, 3, 2), (2, 2))
HELD = (0, 1)
damp_share = 0.01
f32 = jnp.float32
bf16 = jnp.bfloat16
VMEM = pl.BlockSpec(memory_space=pltpu.VMEM)
SMEM = pl.BlockSpec(memory_space=pltpu.SMEM)
LIMIT = pltpu.CompilerParams(vmem_limit_bytes=56 * 2**20)


def split(x):
    high = x.astype(bf16)
    rest = x - high.astype(f32)
    middle = rest.astype(bf16)
    return high, middle, (rest - middle.astype(f32)).astype(bf16)


def left_terms(x, axis=1):
    h, m, l = split(x)
    return jnp.concatenate([h, h, m, m, h, l], axis)


def right_terms(x, axis=1):
    h, m, l = split(x)
    return jnp.concatenate([h, m, h, m, l, h], axis)


def dot(a, b, contract):
    return lax.dot_general(a, b, (contract, ((), ())), preferred_element_type=f32)


def dot_nt(a, b):
    return dot(left_terms(a), right_terms(b), ((1,), (1,)))


def dot_nn(a, b):
    return dot(left_terms(a), right_terms(b, 0), ((1,), (0,)))


def over_lanes(x, j):
    return jnp.broadcast_to(x[:, j : j + 1], (8, 128))


def over_rows(x, i):
    return jnp.broadcast_to(x[i : i + 1, :], x.shape)


def eliminate(rows):
    count = len(rows)
    wide = lambda v: jnp.concatenate([v, v], axis=1)
    rows = list(rows)
    sub = lax.broadcasted_iota(jnp.int32, (8, 128), 0)
    for m in range(count):
        group = rows[m]
        cols = [over_lanes(group, 8 * m + l) for l in range(8)]
        cell = [[over_rows(cols[l], i) if i >= l else None for l in range(8)] for i in range(8)]
        below = [[over_lanes(rows[t], 8 * m + l) for l in range(8)] for t in range(m + 1, count)]
        inverse, diagonal = [], None
        ratio = [[None] * 8 for _ in range(8)]
        for j in range(8):
            d = cell[j][j]
            r = pl.reciprocal(d, approx=True)
            inverse.append(r)
            diagonal = d if diagonal is None else jnp.where(sub == j, d, diagonal)
            pairs = [(i, l) for i in range(j + 1, 8) for l in range(j + 1, i + 1)]
            products = [cell[i][j] * cell[l][j] for i, l in pairs]
            for (i, l), product in zip(pairs, products):
                cell[i][l] = cell[i][l] - product * r
            for l in range(j + 1, 8):
                ratio[l][j] = cell[l][j] * r
        pivots = []
        for j in range(8):
            pivot = over_rows(group, j)
            pivots.append(pivot)
            group = group - wide(jnp.where(sub > j, cols[j] * inverse[j], 0.0)) * pivot
            for l in range(j + 1, 8):
                cols[l] = cols[l] - cols[j] * ratio[l][j]
        rows[m] = group * wide(lax.rsqrt(diagonal))
        for b, t in zip(below, range(m + 1, count)):
            for j in range(8):
                for l in range(j + 1, 8):
                    b[l] = b[l] - b[j] * ratio[l][j]
            terms = [wide(b[j] * inverse[j]) * pivots[j] for j in range(8)]
            while len(terms) > 1:
                terms = [terms[2 * i] + terms[2 * i + 1] for i in range(len(terms) // 2)]
            rows[t] = rows[t] - terms[0]
    return rows


def identity(size):
    return (
        lax.broadcasted_iota(jnp.int32, (size, size), 0) == lax.broadcasted_iota(jnp.int32, (size, size), 1)
    ).astype(f32)


def section_kernel(bounds, here, last, share, damp_ref, *refs):
    first, end = bounds[here], bounds[here + 1]
    span = end - first
    scale_ref, spot_ref, mine_ref, other_ref = refs[:4]
    lower_refs, inverse_refs = refs[4 : 4 + here], refs[4 + here : 4 + 2 * here]
    refs = refs[4 + 2 * here :]
    if last:
        out_ref, work, tile_inverse, gram_ref, lower_ref = refs
        full_inverse = None
    else:
        lower_ref, full_inverse, work, tile_inverse, gram_ref = refs
    half = span // 2
    core = spot_ref[1]
    gram_ref[pl.ds(pl.multiple_of(core * half, half), half), :] = mine_ref[...]
    gram_ref[pl.ds(pl.multiple_of((1 - core) * half, half), half), :] = other_ref[...]
    diag = gram_ref[:, first:end] + damp_ref[0] * identity(span)
    rest = [gram_ref[:, bounds[i] : bounds[i + 1]] for i in range(here)]
    for i in range(here):
        solved = dot_nt(rest[i], inverse_refs[i][...])
        lower_ref[:, bounds[i] : bounds[i + 1]] = solved
        solved_terms = left_terms(solved)
        for n in range(i + 1, here):
            other = right_terms(lower_refs[n][:, bounds[i] : bounds[i + 1]])
            rest[n] = rest[n] - dot(solved_terms, other, ((1,), (1,)))
        diag = diag - dot(solved_terms, right_terms(solved), ((1,), (1,)))
    work[...] = diag
    eye = identity(WIDTH)
    steps = span // WIDTH

    def step(k, carry):
        start = pl.multiple_of(k * WIDTH, WIDTH)
        rows = [
            jnp.concatenate([work[pl.ds(start + t, 8), pl.ds(start, WIDTH)], eye[t : t + 8]], 1)
            for t in range(0, WIDTH, 8)
        ]
        for t, row in enumerate(eliminate(rows)):
            tile_inverse[pl.ds(start + 8 * t, 8), :] = row[:, WIDTH:]
        inverse_terms = right_terms(tile_inverse[pl.ds(start, WIDTH), :])
        for k_here in range(steps):

            @pl.when(k == k_here)
            def _(k_here=k_here):
                top = k_here * WIDTH
                below = top + WIDTH
                panel = dot(left_terms(work[top:, top:below]), inverse_terms, ((1,), (1,)))
                work[top:, top:below] = panel
                if below < span:
                    work[below:, below:] -= dot(
                        left_terms(panel[WIDTH:]), right_terms(panel[WIDTH:]), ((1,), (1,))
                    )

        return carry

    lax.fori_loop(0, steps, step, 0)
    keep = lax.broadcasted_iota(jnp.int32, (span, span), 0) >= lax.broadcasted_iota(jnp.int32, (span, span), 1)
    lower = jnp.where(keep, work[...], 0.0)
    lower_ref[:, first:end] = lower
    if full_inverse is not None:
        whole = tile_inverse[:WIDTH, :]
        for k in range(1, steps):
            top = k * WIDTH
            tile = tile_inverse[top : top + WIDTH, :]
            corner = -dot_nn(tile, dot_nn(lower[top : top + WIDTH, :top], whole))
            whole = jnp.concatenate(
                [
                    jnp.concatenate([whole, jnp.zeros((top, WIDTH), f32)], 1),
                    jnp.concatenate([corner, tile], 1),
                ],
                0,
            )
        full_inverse[...] = whole
    else:
        scale = scale_ref[0]
        place = spot_ref[0]
        sources = list(lower_refs) + [lower_ref]
        for p in range(bounds[-1] // share):

            @pl.when(place == p)
            def _(p=p):
                for i, source in enumerate(sources):
                    low, high = max(bounds[i], p * share), min(bounds[i + 1], (p + 1) * share)
                    if low < high:
                        cols = bounds[i + 1]
                        out_ref[low - p * share : high - p * share, :cols] = (
                            source[low - bounds[i] : high - bounds[i], :] * scale
                        )
                        if cols < bounds[-1]:
                            out_ref[low - p * share : high - p * share, cols:] = jnp.zeros(
                                (high - low, bounds[-1] - cols), f32
                            )


def factor_section(bounds, here, share, damping, scale, spot, mine, other, lowers, inverses):
    span = bounds[here + 1] - bounds[here]
    last = here == len(bounds) - 2
    lower_shape = jax.ShapeDtypeStruct((span, bounds[here + 1]), f32)
    scratch = [
        pltpu.VMEM((span, span), f32),
        pltpu.VMEM((span, WIDTH), f32),
        pltpu.VMEM(lower_shape.shape, f32),
    ]
    if last:
        out_shape = jax.ShapeDtypeStruct((share, bounds[-1]), f32)
        scratch.append(pltpu.VMEM(lower_shape.shape, f32))
    else:
        out_shape = (lower_shape, jax.ShapeDtypeStruct((span, span), f32))
    return pl.pallas_call(
        functools.partial(section_kernel, bounds, here, last, share),
        out_shape=out_shape,
        in_specs=[SMEM] * 3 + [VMEM] * (2 + 2 * here),
        out_specs=VMEM if last else (VMEM, VMEM),
        scratch_shapes=scratch,
        compiler_params=LIMIT,
        cost_estimate=pl.CostEstimate(flops=WIDTH * span, bytes_accessed=span, transcendentals=0),
        name="factor_section",
    )(damping, scale, spot, mine, other, *lowers, *inverses)


def route_kernel(tokens, top_k, owners, capacity, ids_ref, source_ref, count_ref):
    blocks = tokens // 128
    owner = lax.broadcasted_iota(jnp.int32, (owners, 128), 0) * EXP_DEV
    position = lax.broadcasted_iota(jnp.int32, (owners, 128), 1).astype(f32)
    slot = lax.broadcasted_iota(jnp.int32, (capacity, 128), 0).astype(f32)
    row = lax.broadcasted_iota(jnp.int32, (128, 256), 0)
    col = lax.broadcasted_iota(jnp.int32, (128, 256), 1)
    earlier_and_all = jnp.where((row < col) | (col >= 128), 1.0, 0.0).astype(bf16)
    carry = jnp.zeros((owners, 128), f32)
    found = jnp.zeros((3 * owners, capacity), f32)
    for k in range(top_k):
        chosen = [
            jnp.where(
                jnp.broadcast_to(ids_ref[k : k + 1, b * 128 : (b + 1) * 128], (owners, 128)) == owner, 1.0, 0.0
            )
            for b in range(blocks)
        ]
        sums = dot(jnp.concatenate(chosen, 0).astype(bf16), earlier_and_all, ((1,), (0,)))
        marks, slots = [], []
        for b in range(blocks):
            ones = chosen[b]
            part = sums[b * owners : (b + 1) * owners]
            rank = jnp.sum(ones * (part[:, :128] + carry), axis=0, keepdims=True)
            carry = carry + part[:, 128:]
            marks.append(jnp.concatenate([ones, ones * position, ones * float(b * top_k + k)], 0).astype(bf16))
            slots.append(jnp.where(jnp.broadcast_to(rank, (capacity, 128)) == slot, 1.0, 0.0).astype(bf16))
        found = found + dot(jnp.concatenate(marks, 1), jnp.concatenate(slots, 1), ((1,), (1,)))
    filled = found[:owners] > 0.5
    place = found[owners : 2 * owners].astype(jnp.int32)
    block = found[2 * owners :].astype(jnp.int32)
    flat = (block // top_k) * (128 * top_k) + block % top_k + place * top_k
    source_ref[...] = jnp.where(filled, flat, -1)
    count_ref[...] = carry


def route(expert_ids, owners, capacity):
    tokens, top_k = expert_ids.shape
    source, count = pl.pallas_call(
        functools.partial(route_kernel, tokens, top_k, owners, capacity),
        out_shape=(jax.ShapeDtypeStruct((owners, capacity), jnp.int32), jax.ShapeDtypeStruct((owners, 128), f32)),
        in_specs=[VMEM],
        out_specs=(VMEM, VMEM),
        compiler_params=LIMIT,
        name="route",
    )(expert_ids.T)
    return source, count[:, 0]


def swap_groups():
    groups = []
    for x_lo in range(2):
        for core in range(2):
            groups.append([(2 * (x_lo ^ (e % 2)) + core) * 32 + e for e in range(32)])
    return groups


def after(value, *others):
    return lax.optimization_barrier((value, *others))[0]


def shards(hidden, expert_ids):
    tokens_here, top_k, features = hidden.shape
    owners = lax.axis_size("expert")
    parts = lax.axis_size("dp")
    share = features // parts
    capacity = 3 * tokens_here * top_k // (2 * EXP_DEV * owners)
    bounds = [0]
    for sections in CHUNKS:
        for s in sections:
            bounds.append(bounds[-1] + s * WIDTH)
    source, counts = route(expert_ids, owners, capacity)
    slots = source.reshape(-1)
    used = (slots >= 0)[:, None]
    taken = hidden.reshape(-1, features).at[jnp.maximum(slots, 0)].get(mode="promise_in_bounds")
    place = lax.axis_index("dp")
    core = place % 2
    spot = jnp.stack([place, core]).astype(jnp.int32)
    groups = swap_groups()

    pieces, low = [], 0
    for sections in CHUNKS:
        high = low + WIDTH * sum(sections)
        pieces.append(jnp.where(used, taken[:, low:high], jnp.zeros((), bf16)).reshape(owners, capacity, -1))
        low = high
    def send(piece):
        return lax.all_to_all(
            piece, ("dp", "expert"), split_axis=0, concat_axis=0, tiled=True, axis_index_groups=groups
        )

    received, half_sums, swaps, pair_sums, lowers, inverses = [], [], [], {}, [], []

    def sum_grams(rows, sections, whole):
        earlier = list(received)
        received.append(rows)
        first = sum(r.shape[1] for r in earlier)

        def gram_of(low, high):
            parts_here = [
                lax.dot_general(
                    rows[:, low:high], against, (((0,), (0,)), ((), ())), preferred_element_type=f32
                )
                for against in earlier + [rows[:, :high]]
            ]
            return jnp.concatenate(parts_here, 1) if earlier else parts_here[0]

        everything = gram_of(0, rows.shape[1]) if whole else None
        other = None
        for _ in sections:
            c = len(half_sums)
            low, high = bounds[c] - first, bounds[c + 1] - first
            if other is not None and not whole:
                rows = after(rows, other)
            gram = everything[low:high, : bounds[c + 1]] if whole else gram_of(low, high)
            half = gram.shape[0] // 2
            mine = lax.dynamic_slice_in_dim(gram, core * half, half, 0)
            other = lax.dynamic_slice_in_dim(gram, (1 - core) * half, half, 0)
            half_sums.append(mine + lax.ppermute(other, "dp", [(i, i ^ 1) for i in range(parts)]))

    def swap_halves():
        while len(swaps) < len(half_sums):
            half_sum = half_sums[len(swaps)]
            if len(swaps) == 1:
                half_sum = after(half_sum, swaps[0])
            swaps.append(lax.ppermute(half_sum, "dp", [(i, i ^ 2) for i in range(parts)]))

    def pair_sum(c):
        if c not in pair_sums:
            mine = half_sums[c] + after(swaps[c], *lowers[-1:])
            pair_sums[c] = mine, lax.ppermute(mine, "dp", [(i, i ^ 1) for i in range(parts)])
        return pair_sums[c]

    def factor(c):
        mine, other = pair_sum(c)
        mine = after(mine, *half_sums[c + 1 :])
        result = factor_section(bounds, c, share, damping, scale, spot, mine, other, lowers, inverses)
        if c < len(bounds) - 2:
            lowers.append(result[0])
            inverses.append(result[1])
        return result

    sent = send(pieces[0])
    squares = jnp.where(used, jnp.square(taken.astype(f32)), 0.0).reshape(owners, -1)
    facts = jnp.stack([counts, jnp.sum(squares, axis=1)], 1)
    sent = after(sent, facts, pieces[1])
    facts = jnp.tile(after(facts, sent), (parts, 1))
    facts = lax.all_to_all(facts, ("dp", "expert"), split_axis=0, concat_axis=0, tiled=True)
    total = jnp.sum(facts, axis=0)
    scale = jnp.sqrt(2.0 / total[0])[None]
    damping = (damp_share * total[1] / features)[None]
    sum_grams(sent.reshape(owners * capacity, -1), CHUNKS[0], False)
    swap_halves()
    pieces[1] = after(pieces[1], facts)
    for chunk in range(1, len(CHUNKS)):
        sent = send(after(pieces[chunk], sent))
        done = len(half_sums) - HELD[chunk]
        while len(lowers) < done:
            factor(len(lowers))
        ready = lowers[-1:]
        if len(lowers) < len(half_sums):
            ready = ready + [pair_sum(len(lowers))[0]]
        rows = after(sent, *ready)
        sum_grams(rows.reshape(owners * capacity, -1), CHUNKS[chunk], True)
        swap_halves()
    while len(lowers) < len(half_sums) - 1:
        factor(len(lowers))
    return factor(len(lowers))[None]


def solution(mesh):
    placed = (P(("dp", "expert"), None, None), P(("dp", "expert"), None))
    return jax.shard_map(
        shards, mesh=mesh, in_specs=placed, out_specs=P("expert", "dp", None), check_vma=False
    )
```

```python
import functools

import jax
import jax.numpy as jnp
from jax import lax
from jax.experimental import pallas as pl
from jax.experimental.pallas import tpu as pltpu
from jax.sharding import PartitionSpec as P

EXP_DEV = 4
WIDTH = 128
CHUNKS = ((3, 3, 2), (2, 2))
HELD = (0, 1)
damp_share = 0.01
f32 = jnp.float32
bf16 = jnp.bfloat16
VMEM = pl.BlockSpec(memory_space=pltpu.VMEM)
SMEM = pl.BlockSpec(memory_space=pltpu.SMEM)
LIMIT = pltpu.CompilerParams(vmem_limit_bytes=56 * 2**20)


def split(x):
    high = x.astype(bf16)
    rest = x - high.astype(f32)
    middle = rest.astype(bf16)
    return high, middle, (rest - middle.astype(f32)).astype(bf16)


def left_terms(x, axis=1):
    h, m, l = split(x)
    return jnp.concatenate([h, h, m, m, h, l], axis)


def right_terms(x, axis=1):
    h, m, l = split(x)
    return jnp.concatenate([h, m, h, m, l, h], axis)


def dot(a, b, contract):
    return lax.dot_general(a, b, (contract, ((), ())), preferred_element_type=f32)


def dot_nt(a, b):
    return dot(left_terms(a), right_terms(b), ((1,), (1,)))


def dot_nn(a, b):
    return dot(left_terms(a), right_terms(b, 0), ((1,), (0,)))


def over_lanes(x, j):
    return jnp.broadcast_to(x[:, j : j + 1], (8, 128))


def over_rows(x, i):
    return jnp.broadcast_to(x[i : i + 1, :], x.shape)


def eliminate(rows):
    count = len(rows)
    wide = lambda v: jnp.concatenate([v, v], axis=1)
    rows = list(rows)
    sub = lax.broadcasted_iota(jnp.int32, (8, 128), 0)
    for m in range(count):
        group = rows[m]
        cols = [over_lanes(group, 8 * m + l) for l in range(8)]
        cell = [[over_rows(cols[l], i) if i >= l else None for l in range(8)] for i in range(8)]
        below = [[over_lanes(rows[t], 8 * m + l) for l in range(8)] for t in range(m + 1, count)]
        inverse, diagonal = [], None
        ratio = [[None] * 8 for _ in range(8)]
        for j in range(8):
            d = cell[j][j]
            r = pl.reciprocal(d, approx=True)
            inverse.append(r)
            diagonal = d if diagonal is None else jnp.where(sub == j, d, diagonal)
            pairs = [(i, l) for i in range(j + 1, 8) for l in range(j + 1, i + 1)]
            products = [cell[i][j] * cell[l][j] for i, l in pairs]
            for (i, l), product in zip(pairs, products):
                cell[i][l] = cell[i][l] - product * r
            for l in range(j + 1, 8):
                ratio[l][j] = cell[l][j] * r
        pivots = []
        for j in range(8):
            pivot = over_rows(group, j)
            pivots.append(pivot)
            group = group - wide(jnp.where(sub > j, cols[j] * inverse[j], 0.0)) * pivot
            for l in range(j + 1, 8):
                cols[l] = cols[l] - cols[j] * ratio[l][j]
        rows[m] = group * wide(lax.rsqrt(diagonal))
        for b, t in zip(below, range(m + 1, count)):
            for j in range(8):
                for l in range(j + 1, 8):
                    b[l] = b[l] - b[j] * ratio[l][j]
            terms = [wide(b[j] * inverse[j]) * pivots[j] for j in range(8)]
            while len(terms) > 1:
                terms = [terms[2 * i] + terms[2 * i + 1] for i in range(len(terms) // 2)]
            rows[t] = rows[t] - terms[0]
    return rows


def identity(size):
    return (
        lax.broadcasted_iota(jnp.int32, (size, size), 0) == lax.broadcasted_iota(jnp.int32, (size, size), 1)
    ).astype(f32)


def section_kernel(bounds, here, last, share, damp_ref, *refs):
    first, end = bounds[here], bounds[here + 1]
    span = end - first
    scale_ref, spot_ref, mine_ref, other_ref = refs[:4]
    lower_refs, inverse_refs = refs[4 : 4 + here], refs[4 + here : 4 + 2 * here]
    refs = refs[4 + 2 * here :]
    if last:
        out_ref, work, tile_inverse, gram_ref, lower_ref = refs
        full_inverse = None
    else:
        lower_ref, full_inverse, work, tile_inverse, gram_ref = refs
    half = span // 2
    core = spot_ref[1]
    gram_ref[pl.ds(pl.multiple_of(core * half, half), half), :] = mine_ref[...]
    gram_ref[pl.ds(pl.multiple_of((1 - core) * half, half), half), :] = other_ref[...]
    diag = gram_ref[:, first:end] + damp_ref[0] * identity(span)
    rest = [gram_ref[:, bounds[i] : bounds[i + 1]] for i in range(here)]
    for i in range(here):
        solved = dot_nt(rest[i], inverse_refs[i][...])
        lower_ref[:, bounds[i] : bounds[i + 1]] = solved
        solved_terms = left_terms(solved)
        for n in range(i + 1, here):
            other = right_terms(lower_refs[n][:, bounds[i] : bounds[i + 1]])
            rest[n] = rest[n] - dot(solved_terms, other, ((1,), (1,)))
        diag = diag - dot(solved_terms, right_terms(solved), ((1,), (1,)))
    work[...] = diag
    eye = identity(WIDTH)
    steps = span // WIDTH

    def step(k, carry):
        start = pl.multiple_of(k * WIDTH, WIDTH)
        rows = [
            jnp.concatenate([work[pl.ds(start + t, 8), pl.ds(start, WIDTH)], eye[t : t + 8]], 1)
            for t in range(0, WIDTH, 8)
        ]
        for t, row in enumerate(eliminate(rows)):
            tile_inverse[pl.ds(start + 8 * t, 8), :] = row[:, WIDTH:]
        inverse_terms = right_terms(tile_inverse[pl.ds(start, WIDTH), :])
        for k_here in range(steps):

            @pl.when(k == k_here)
            def _(k_here=k_here):
                top = k_here * WIDTH
                below = top + WIDTH
                panel = dot(left_terms(work[top:, top:below]), inverse_terms, ((1,), (1,)))
                work[top:, top:below] = panel
                if below < span:
                    work[below:, below:] -= dot(
                        left_terms(panel[WIDTH:]), right_terms(panel[WIDTH:]), ((1,), (1,))
                    )

        return carry

    lax.fori_loop(0, steps, step, 0)
    keep = lax.broadcasted_iota(jnp.int32, (span, span), 0) >= lax.broadcasted_iota(jnp.int32, (span, span), 1)
    lower = jnp.where(keep, work[...], 0.0)
    lower_ref[:, first:end] = lower
    if full_inverse is not None:
        whole = tile_inverse[:WIDTH, :]
        for k in range(1, steps):
            top = k * WIDTH
            tile = tile_inverse[top : top + WIDTH, :]
            corner = -dot_nn(tile, dot_nn(lower[top : top + WIDTH, :top], whole))
            whole = jnp.concatenate(
                [
                    jnp.concatenate([whole, jnp.zeros((top, WIDTH), f32)], 1),
                    jnp.concatenate([corner, tile], 1),
                ],
                0,
            )
        full_inverse[...] = whole
    else:
        scale = scale_ref[0]
        place = spot_ref[0]
        sources = list(lower_refs) + [lower_ref]
        for p in range(bounds[-1] // share):

            @pl.when(place == p)
            def _(p=p):
                for i, source in enumerate(sources):
                    low, high = max(bounds[i], p * share), min(bounds[i + 1], (p + 1) * share)
                    if low < high:
                        cols = bounds[i + 1]
                        out_ref[low - p * share : high - p * share, :cols] = (
                            source[low - bounds[i] : high - bounds[i], :] * scale
                        )
                        if cols < bounds[-1]:
                            out_ref[low - p * share : high - p * share, cols:] = jnp.zeros(
                                (high - low, bounds[-1] - cols), f32
                            )


def factor_section(bounds, here, share, damping, scale, spot, mine, other, lowers, inverses):
    span = bounds[here + 1] - bounds[here]
    last = here == len(bounds) - 2
    lower_shape = jax.ShapeDtypeStruct((span, bounds[here + 1]), f32)
    scratch = [
        pltpu.VMEM((span, span), f32),
        pltpu.VMEM((span, WIDTH), f32),
        pltpu.VMEM(lower_shape.shape, f32),
    ]
    if last:
        out_shape = jax.ShapeDtypeStruct((share, bounds[-1]), f32)
        scratch.append(pltpu.VMEM(lower_shape.shape, f32))
    else:
        out_shape = (lower_shape, jax.ShapeDtypeStruct((span, span), f32))
    return pl.pallas_call(
        functools.partial(section_kernel, bounds, here, last, share),
        out_shape=out_shape,
        in_specs=[SMEM] * 3 + [VMEM] * (2 + 2 * here),
        out_specs=VMEM if last else (VMEM, VMEM),
        scratch_shapes=scratch,
        compiler_params=LIMIT,
        cost_estimate=pl.CostEstimate(flops=WIDTH * span, bytes_accessed=span, transcendentals=0),
        name="factor_section",
    )(damping, scale, spot, mine, other, *lowers, *inverses)


def route_kernel(tokens, top_k, owners, capacity, ids_ref, source_ref, count_ref):
    blocks = tokens // 128
    owner = lax.broadcasted_iota(jnp.int32, (owners, 128), 0) * EXP_DEV
    position = lax.broadcasted_iota(jnp.int32, (owners, 128), 1).astype(f32)
    slot = lax.broadcasted_iota(jnp.int32, (capacity, 128), 0).astype(f32)
    row = lax.broadcasted_iota(jnp.int32, (128, 256), 0)
    col = lax.broadcasted_iota(jnp.int32, (128, 256), 1)
    earlier_and_all = jnp.where((row < col) | (col >= 128), 1.0, 0.0).astype(bf16)
    carry = jnp.zeros((owners, 128), f32)
    found = jnp.zeros((3 * owners, capacity), f32)
    for k in range(top_k):
        chosen = [
            jnp.where(
                jnp.broadcast_to(ids_ref[k : k + 1, b * 128 : (b + 1) * 128], (owners, 128)) == owner, 1.0, 0.0
            )
            for b in range(blocks)
        ]
        sums = dot(jnp.concatenate(chosen, 0).astype(bf16), earlier_and_all, ((1,), (0,)))
        marks, slots = [], []
        for b in range(blocks):
            ones = chosen[b]
            part = sums[b * owners : (b + 1) * owners]
            rank = jnp.sum(ones * (part[:, :128] + carry), axis=0, keepdims=True)
            carry = carry + part[:, 128:]
            marks.append(jnp.concatenate([ones, ones * position, ones * float(b * top_k + k)], 0).astype(bf16))
            slots.append(jnp.where(jnp.broadcast_to(rank, (capacity, 128)) == slot, 1.0, 0.0).astype(bf16))
        found = found + dot(jnp.concatenate(marks, 1), jnp.concatenate(slots, 1), ((1,), (1,)))
    filled = found[:owners] > 0.5
    place = found[owners : 2 * owners].astype(jnp.int32)
    block = found[2 * owners :].astype(jnp.int32)
    flat = (block // top_k) * (128 * top_k) + block % top_k + place * top_k
    source_ref[...] = jnp.where(filled, flat, -1)
    count_ref[...] = carry


def route(expert_ids, owners, capacity):
    tokens, top_k = expert_ids.shape
    source, count = pl.pallas_call(
        functools.partial(route_kernel, tokens, top_k, owners, capacity),
        out_shape=(jax.ShapeDtypeStruct((owners, capacity), jnp.int32), jax.ShapeDtypeStruct((owners, 128), f32)),
        in_specs=[VMEM],
        out_specs=(VMEM, VMEM),
        compiler_params=LIMIT,
        name="route",
    )(expert_ids.T)
    return source, count


def pack_kernel(first, group, capacity, count_ref, taken_ref, head_ref, tail_ref):
    features = taken_ref.shape[1]
    row = lax.broadcasted_iota(jnp.int32, (capacity, features), 0).astype(f32)
    lane = lax.broadcasted_iota(jnp.int32, (8, first), 1)
    top = lax.broadcasted_iota(jnp.int32, (8, first), 0) == 0
    for g in range(group):
        count = count_ref[g : g + 1, :1]
        rows = taken_ref[g * capacity : (g + 1) * capacity, :].astype(f32)
        rows = jnp.where(row < jnp.broadcast_to(count, row.shape), rows, 0.0)
        squares = jnp.full((8, first), jnp.sum(rows * rows), f32)
        facts = jnp.where(lane == 0, jnp.broadcast_to(count, (8, first)), 0.0)
        for i, term in enumerate(split(squares)):
            facts = jnp.where(lane == i + 1, term.astype(f32), facts)
        facts = jnp.where(top, facts, 0.0)
        head_ref[g] = jnp.concatenate([rows[:, :first], facts], 0).astype(bf16)
        tail_ref[g] = rows[:, first:].astype(bf16)


def pack(taken, counts, first):
    owners = counts.shape[0]
    capacity = taken.shape[0] // owners
    features = taken.shape[1]
    group = 8
    return pl.pallas_call(
        functools.partial(pack_kernel, first, group, capacity),
        grid=(owners // group,),
        out_shape=(
            jax.ShapeDtypeStruct((owners, capacity + 8, first), bf16),
            jax.ShapeDtypeStruct((owners, capacity, features - first), bf16),
        ),
        in_specs=[
            pl.BlockSpec((group, 128), lambda i: (i, 0)),
            pl.BlockSpec((group * capacity, features), lambda i: (i, 0)),
        ],
        out_specs=(
            pl.BlockSpec((group, capacity + 8, first), lambda i: (i, 0, 0)),
            pl.BlockSpec((group, capacity, features - first), lambda i: (i, 0, 0)),
        ),
        compiler_params=LIMIT,
        name="pack",
    )(counts, taken)


def swap_groups():
    groups = []
    for x_lo in range(2):
        for core in range(2):
            groups.append([(2 * (x_lo ^ (e % 2)) + core) * 32 + e for e in range(32)])
    return groups


def after(value, *others):
    return lax.optimization_barrier((value, *others))[0]


def shards(hidden, expert_ids):
    tokens_here, top_k, features = hidden.shape
    owners = lax.axis_size("expert")
    parts = lax.axis_size("dp")
    share = features // parts
    capacity = 3 * tokens_here * top_k // (2 * EXP_DEV * owners)
    bounds = [0]
    for sections in CHUNKS:
        for s in sections:
            bounds.append(bounds[-1] + s * WIDTH)
    source, counts = route(expert_ids, owners, capacity)
    slots = source.reshape(-1)
    taken = hidden.reshape(-1, features).at[jnp.maximum(slots, 0)].get(mode="promise_in_bounds")
    place = lax.axis_index("dp")
    core = place % 2
    spot = jnp.stack([place, core]).astype(jnp.int32)
    groups = swap_groups()

    pieces = list(pack(taken, counts, WIDTH * sum(CHUNKS[0])))

    def send(piece):
        return lax.all_to_all(
            piece, ("dp", "expert"), split_axis=0, concat_axis=0, tiled=True, axis_index_groups=groups
        )

    scalars = {}
    received, half_sums, swaps, pair_sums, lowers, inverses = [], [], [], {}, [], []

    def sum_grams(rows, sections, whole):
        earlier = list(received)
        received.append(rows)
        first = sum(r.shape[1] for r in earlier)

        def gram_of(low, high):
            parts_here = [
                lax.dot_general(
                    rows[:, low:high], against, (((0,), (0,)), ((), ())), preferred_element_type=f32
                )
                for against in earlier + [rows[:, :high]]
            ]
            return jnp.concatenate(parts_here, 1) if earlier else parts_here[0]

        everything = gram_of(0, rows.shape[1]) if whole else None
        other = None
        for _ in sections:
            c = len(half_sums)
            low, high = bounds[c] - first, bounds[c + 1] - first
            if other is not None and not whole:
                rows = after(rows, other)
            gram = everything[low:high, : bounds[c + 1]] if whole else gram_of(low, high)
            half = gram.shape[0] // 2
            mine = lax.dynamic_slice_in_dim(gram, core * half, half, 0)
            other = lax.dynamic_slice_in_dim(gram, (1 - core) * half, half, 0)
            if c == 0:
                mine = jnp.concatenate([mine, facts], 0)
                other = jnp.concatenate([other, facts], 0)
            half_sums.append(mine + lax.ppermute(other, "dp", [(i, i ^ 1) for i in range(parts)]))

    def swap_halves():
        while len(swaps) < len(half_sums):
            half_sum = half_sums[len(swaps)]
            if len(swaps) == 1:
                half_sum = after(half_sum, swaps[0])
            swaps.append(lax.ppermute(half_sum, "dp", [(i, i ^ 2) for i in range(parts)]))

    def pair_sum(c):
        if c not in pair_sums:
            mine = half_sums[c] + after(swaps[c], *lowers[-1:])
            if c == 0:
                total = mine[-8, :2]
                scalars["scale"] = jnp.sqrt(2.0 / total[:1])
                scalars["damping"] = damp_share * total[1:] / features
                mine = mine[:-8]
            pair_sums[c] = mine, lax.ppermute(mine, "dp", [(i, i ^ 1) for i in range(parts)])
        return pair_sums[c]

    def factor(c):
        mine, other = pair_sum(c)
        mine = after(mine, *half_sums[c + 1 :])
        result = factor_section(bounds, c, share, scalars["damping"], scalars["scale"], spot, mine, other, lowers, inverses)
        if c < len(bounds) - 2:
            lowers.append(result[0])
            inverses.append(result[1])
        return result

    sent = send(pieces[0])
    told = jnp.sum(sent[:, capacity, :4].astype(f32), axis=0)
    facts = jnp.stack([told[0], told[1] + told[2] + told[3]])
    facts = jnp.pad(facts[None], ((0, 7), (0, WIDTH * CHUNKS[0][0] - 2)))
    sum_grams(sent[:, :capacity].reshape(owners * capacity, -1), CHUNKS[0], False)
    swap_halves()
    for chunk in range(1, len(CHUNKS)):
        sent = send(after(pieces[chunk], sent))
        done = len(half_sums) - HELD[chunk]
        while len(lowers) < done:
            factor(len(lowers))
        ready = lowers[-1:]
        if len(lowers) < len(half_sums):
            ready = ready + [pair_sum(len(lowers))[0]]
        rows = after(sent, *ready)
        sum_grams(rows.reshape(owners * capacity, -1), CHUNKS[chunk], True)
        swap_halves()
    while len(lowers) < len(half_sums) - 1:
        factor(len(lowers))
    return factor(len(lowers))[None]


def solution(mesh):
    placed = (P(("dp", "expert"), None, None), P(("dp", "expert"), None))
    return jax.shard_map(
        shards, mesh=mesh, in_specs=placed, out_specs=P("expert", "dp", None), check_vma=False
    )
```

```python
import functools

import jax
import jax.numpy as jnp
from jax import lax
from jax.experimental import pallas as pl
from jax.experimental.pallas import tpu as pltpu
from jax.sharding import PartitionSpec as P

EXP_DEV = 4
WIDTH = 128
CHUNKS = ((3, 3, 2), (2, 2))
HELD = (0, 1)
damp_share = 0.01
f32 = jnp.float32
bf16 = jnp.bfloat16
VMEM = pl.BlockSpec(memory_space=pltpu.VMEM)
SMEM = pl.BlockSpec(memory_space=pltpu.SMEM)
LIMIT = pltpu.CompilerParams(vmem_limit_bytes=56 * 2**20)


def split(x):
    high = x.astype(bf16)
    rest = x - high.astype(f32)
    middle = rest.astype(bf16)
    return high, middle, (rest - middle.astype(f32)).astype(bf16)


def left_terms(x, axis=1):
    h, m, l = split(x)
    return jnp.concatenate([h, h, m, m, h, l], axis)


def right_terms(x, axis=1):
    h, m, l = split(x)
    return jnp.concatenate([h, m, h, m, l, h], axis)


def dot(a, b, contract):
    return lax.dot_general(a, b, (contract, ((), ())), preferred_element_type=f32)


def dot_nt(a, b):
    return dot(left_terms(a), right_terms(b), ((1,), (1,)))


def dot_nn(a, b):
    return dot(left_terms(a), right_terms(b, 0), ((1,), (0,)))


def over_lanes(x, j):
    return jnp.broadcast_to(x[:, j : j + 1], (8, 128))


def over_rows(x, i):
    return jnp.broadcast_to(x[i : i + 1, :], x.shape)


def eliminate(rows):
    count = len(rows)
    wide = lambda v: jnp.concatenate([v, v], axis=1)
    rows = list(rows)
    sub = lax.broadcasted_iota(jnp.int32, (8, 128), 0)
    for m in range(count):
        group = rows[m]
        cols = [over_lanes(group, 8 * m + l) for l in range(8)]
        cell = [[over_rows(cols[l], i) if i >= l else None for l in range(8)] for i in range(8)]
        below = [[over_lanes(rows[t], 8 * m + l) for l in range(8)] for t in range(m + 1, count)]
        inverse, diagonal = [], None
        ratio = [[None] * 8 for _ in range(8)]
        for j in range(8):
            d = cell[j][j]
            r = pl.reciprocal(d, approx=True)
            inverse.append(r)
            diagonal = d if diagonal is None else jnp.where(sub == j, d, diagonal)
            pairs = [(i, l) for i in range(j + 1, 8) for l in range(j + 1, i + 1)]
            products = [cell[i][j] * cell[l][j] for i, l in pairs]
            for (i, l), product in zip(pairs, products):
                cell[i][l] = cell[i][l] - product * r
            for l in range(j + 1, 8):
                ratio[l][j] = cell[l][j] * r
        pivots = []
        for j in range(8):
            pivot = over_rows(group, j)
            pivots.append(pivot)
            group = group - wide(jnp.where(sub > j, cols[j] * inverse[j], 0.0)) * pivot
            for l in range(j + 1, 8):
                cols[l] = cols[l] - cols[j] * ratio[l][j]
        rows[m] = group * wide(lax.rsqrt(diagonal))
        for b, t in zip(below, range(m + 1, count)):
            for j in range(8):
                for l in range(j + 1, 8):
                    b[l] = b[l] - b[j] * ratio[l][j]
            terms = [wide(b[j] * inverse[j]) * pivots[j] for j in range(8)]
            while len(terms) > 1:
                terms = [terms[2 * i] + terms[2 * i + 1] for i in range(len(terms) // 2)]
            rows[t] = rows[t] - terms[0]
    return rows


def identity(size):
    return (
        lax.broadcasted_iota(jnp.int32, (size, size), 0) == lax.broadcasted_iota(jnp.int32, (size, size), 1)
    ).astype(f32)


def section_kernel(bounds, here, last, share, damp_ref, *refs):
    first, end = bounds[here], bounds[here + 1]
    span = end - first
    scale_ref, spot_ref, mine_ref, other_ref = refs[:4]
    lower_refs, inverse_refs = refs[4 : 4 + here], refs[4 + here : 4 + 2 * here]
    refs = refs[4 + 2 * here :]
    if last:
        out_ref, work, tile_inverse, gram_ref, lower_ref = refs
        full_inverse = None
    else:
        lower_ref, full_inverse, work, tile_inverse, gram_ref = refs
    half = span // 2
    core = spot_ref[1]
    gram_ref[pl.ds(pl.multiple_of(core * half, half), half), :] = mine_ref[...]
    gram_ref[pl.ds(pl.multiple_of((1 - core) * half, half), half), :] = other_ref[...]
    diag = gram_ref[:, first:end] + damp_ref[0] * identity(span)
    rest = [gram_ref[:, bounds[i] : bounds[i + 1]] for i in range(here)]
    for i in range(here):
        solved = dot_nt(rest[i], inverse_refs[i][...])
        lower_ref[:, bounds[i] : bounds[i + 1]] = solved
        solved_terms = left_terms(solved)
        for n in range(i + 1, here):
            other = right_terms(lower_refs[n][:, bounds[i] : bounds[i + 1]])
            rest[n] = rest[n] - dot(solved_terms, other, ((1,), (1,)))
        diag = diag - dot(solved_terms, right_terms(solved), ((1,), (1,)))
    work[...] = diag
    eye = identity(WIDTH)
    steps = span // WIDTH

    def step(k, carry):
        start = pl.multiple_of(k * WIDTH, WIDTH)
        rows = [
            jnp.concatenate([work[pl.ds(start + t, 8), pl.ds(start, WIDTH)], eye[t : t + 8]], 1)
            for t in range(0, WIDTH, 8)
        ]
        for t, row in enumerate(eliminate(rows)):
            tile_inverse[pl.ds(start + 8 * t, 8), :] = row[:, WIDTH:]
        inverse_terms = right_terms(tile_inverse[pl.ds(start, WIDTH), :])
        for k_here in range(steps):

            @pl.when(k == k_here)
            def _(k_here=k_here):
                top = k_here * WIDTH
                below = top + WIDTH
                panel = dot(left_terms(work[top:, top:below]), inverse_terms, ((1,), (1,)))
                work[top:, top:below] = panel
                if below < span:
                    work[below:, below:] -= dot(
                        left_terms(panel[WIDTH:]), right_terms(panel[WIDTH:]), ((1,), (1,))
                    )

        return carry

    lax.fori_loop(0, steps, step, 0)
    keep = lax.broadcasted_iota(jnp.int32, (span, span), 0) >= lax.broadcasted_iota(jnp.int32, (span, span), 1)
    lower = jnp.where(keep, work[...], 0.0)
    lower_ref[:, first:end] = lower
    if full_inverse is not None:
        whole = tile_inverse[:WIDTH, :]
        for k in range(1, steps):
            top = k * WIDTH
            tile = tile_inverse[top : top + WIDTH, :]
            corner = -dot_nn(tile, dot_nn(lower[top : top + WIDTH, :top], whole))
            whole = jnp.concatenate(
                [
                    jnp.concatenate([whole, jnp.zeros((top, WIDTH), f32)], 1),
                    jnp.concatenate([corner, tile], 1),
                ],
                0,
            )
        full_inverse[...] = whole
    else:
        scale = scale_ref[0]
        place = spot_ref[0]
        sources = list(lower_refs) + [lower_ref]
        for p in range(bounds[-1] // share):

            @pl.when(place == p)
            def _(p=p):
                for i, source in enumerate(sources):
                    low, high = max(bounds[i], p * share), min(bounds[i + 1], (p + 1) * share)
                    if low < high:
                        cols = bounds[i + 1]
                        out_ref[low - p * share : high - p * share, :cols] = (
                            source[low - bounds[i] : high - bounds[i], :] * scale
                        )
                        if cols < bounds[-1]:
                            out_ref[low - p * share : high - p * share, cols:] = jnp.zeros(
                                (high - low, bounds[-1] - cols), f32
                            )


def factor_section(bounds, here, share, damping, scale, spot, mine, other, lowers, inverses):
    span = bounds[here + 1] - bounds[here]
    last = here == len(bounds) - 2
    lower_shape = jax.ShapeDtypeStruct((span, bounds[here + 1]), f32)
    scratch = [
        pltpu.VMEM((span, span), f32),
        pltpu.VMEM((span, WIDTH), f32),
        pltpu.VMEM(lower_shape.shape, f32),
    ]
    if last:
        out_shape = jax.ShapeDtypeStruct((share, bounds[-1]), f32)
        scratch.append(pltpu.VMEM(lower_shape.shape, f32))
    else:
        out_shape = (lower_shape, jax.ShapeDtypeStruct((span, span), f32))
    return pl.pallas_call(
        functools.partial(section_kernel, bounds, here, last, share),
        out_shape=out_shape,
        in_specs=[SMEM] * 3 + [VMEM] * (2 + 2 * here),
        out_specs=VMEM if last else (VMEM, VMEM),
        scratch_shapes=scratch,
        compiler_params=LIMIT,
        cost_estimate=pl.CostEstimate(flops=WIDTH * span, bytes_accessed=span, transcendentals=0),
        name="factor_section",
    )(damping, scale, spot, mine, other, *lowers, *inverses)


def route_kernel(tokens, top_k, owners, capacity, ids_ref, source_ref, count_ref):
    blocks = tokens // 128
    owner = lax.broadcasted_iota(jnp.int32, (owners, 128), 0) * EXP_DEV
    position = lax.broadcasted_iota(jnp.int32, (owners, 128), 1).astype(f32)
    slot = lax.broadcasted_iota(jnp.int32, (capacity, 128), 0).astype(f32)
    row = lax.broadcasted_iota(jnp.int32, (128, 256), 0)
    col = lax.broadcasted_iota(jnp.int32, (128, 256), 1)
    earlier_and_all = jnp.where((row < col) | (col >= 128), 1.0, 0.0).astype(bf16)
    carry = jnp.zeros((owners, 128), f32)
    found = jnp.zeros((3 * owners, capacity), f32)
    for k in range(top_k):
        chosen = [
            jnp.where(
                jnp.broadcast_to(ids_ref[k : k + 1, b * 128 : (b + 1) * 128], (owners, 128)) == owner, 1.0, 0.0
            )
            for b in range(blocks)
        ]
        sums = dot(jnp.concatenate(chosen, 0).astype(bf16), earlier_and_all, ((1,), (0,)))
        marks, slots = [], []
        for b in range(blocks):
            ones = chosen[b]
            part = sums[b * owners : (b + 1) * owners]
            rank = jnp.sum(ones * (part[:, :128] + carry), axis=0, keepdims=True)
            carry = carry + part[:, 128:]
            marks.append(jnp.concatenate([ones, ones * position, ones * float(b * top_k + k)], 0).astype(bf16))
            slots.append(jnp.where(jnp.broadcast_to(rank, (capacity, 128)) == slot, 1.0, 0.0).astype(bf16))
        found = found + dot(jnp.concatenate(marks, 1), jnp.concatenate(slots, 1), ((1,), (1,)))
    filled = found[:owners] > 0.5
    place = found[owners : 2 * owners].astype(jnp.int32)
    block = found[2 * owners :].astype(jnp.int32)
    flat = (block // top_k) * (128 * top_k) + block % top_k + place * top_k
    source_ref[...] = jnp.where(filled, flat, -1)
    count_ref[...] = carry


def route(expert_ids, owners, capacity):
    tokens, top_k = expert_ids.shape
    source, count = pl.pallas_call(
        functools.partial(route_kernel, tokens, top_k, owners, capacity),
        out_shape=(jax.ShapeDtypeStruct((owners, capacity), jnp.int32), jax.ShapeDtypeStruct((owners, 128), f32)),
        in_specs=[VMEM],
        out_specs=(VMEM, VMEM),
        compiler_params=LIMIT,
        name="route",
    )(expert_ids.T)
    return source, count[:, 0]


def swap_groups():
    groups = []
    for x_lo in range(2):
        for core in range(2):
            groups.append([(2 * (x_lo ^ (e % 2)) + core) * 32 + e for e in range(32)])
    return groups


def after(value, *others):
    return lax.optimization_barrier((value, *others))[0]


def exchanged(value, stages):
    for axis, mask in stages:
        value = value + lax.ppermute(value, axis, [(i, i ^ mask) for i in range(lax.axis_size(axis))])
    return value


def shards(hidden, expert_ids):
    tokens_here, top_k, features = hidden.shape
    owners = lax.axis_size("expert")
    parts = lax.axis_size("dp")
    share = features // parts
    capacity = 3 * tokens_here * top_k // (2 * EXP_DEV * owners)
    bounds = [0]
    for sections in CHUNKS:
        for s in sections:
            bounds.append(bounds[-1] + s * WIDTH)
    source, counts = route(expert_ids, owners, capacity)
    slots = source.reshape(-1)
    used = (slots >= 0)[:, None]
    taken = hidden.reshape(-1, features).at[jnp.maximum(slots, 0)].get(mode="promise_in_bounds")
    place = lax.axis_index("dp")
    core = place % 2
    spot = jnp.stack([place, core]).astype(jnp.int32)
    groups = swap_groups()

    pieces, low = [], 0
    for sections in CHUNKS:
        high = low + WIDTH * sum(sections)
        pieces.append(jnp.where(used, taken[:, low:high], jnp.zeros((), bf16)).reshape(owners, capacity, -1))
        low = high
    def send(piece):
        return lax.all_to_all(
            piece, ("dp", "expert"), split_axis=0, concat_axis=0, tiled=True, axis_index_groups=groups
        )

    received, half_sums, swaps, pair_sums, lowers, inverses = [], [], [], {}, [], []

    def sum_grams(rows, sections, whole):
        earlier = list(received)
        received.append(rows)
        first = sum(r.shape[1] for r in earlier)

        def gram_of(low, high):
            parts_here = [
                lax.dot_general(
                    rows[:, low:high], against, (((0,), (0,)), ((), ())), preferred_element_type=f32
                )
                for against in earlier + [rows[:, :high]]
            ]
            return jnp.concatenate(parts_here, 1) if earlier else parts_here[0]

        everything = gram_of(0, rows.shape[1]) if whole else None
        other = None
        for _ in sections:
            c = len(half_sums)
            low, high = bounds[c] - first, bounds[c + 1] - first
            if other is not None and not whole:
                rows = after(rows, other)
            gram = everything[low:high, : bounds[c + 1]] if whole else gram_of(low, high)
            half = gram.shape[0] // 2
            mine = lax.dynamic_slice_in_dim(gram, core * half, half, 0)
            other = lax.dynamic_slice_in_dim(gram, (1 - core) * half, half, 0)
            half_sums.append(mine + lax.ppermute(other, "dp", [(i, i ^ 1) for i in range(parts)]))

    def swap_halves():
        while len(swaps) < len(half_sums):
            half_sum = half_sums[len(swaps)]
            if len(swaps) == 1:
                half_sum = after(half_sum, swaps[0])
            swaps.append(lax.ppermute(half_sum, "dp", [(i, i ^ 2) for i in range(parts)]))

    def pair_sum(c):
        if c not in pair_sums:
            mine = half_sums[c] + after(swaps[c], *lowers[-1:])
            pair_sums[c] = mine, lax.ppermute(mine, "dp", [(i, i ^ 1) for i in range(parts)])
        return pair_sums[c]

    def factor(c):
        mine, other = pair_sum(c)
        mine = after(mine, *half_sums[c + 1 :])
        result = factor_section(bounds, c, share, damping, scale, spot, mine, other, lowers, inverses)
        if c < len(bounds) - 2:
            lowers.append(result[0])
            inverses.append(result[1])
        return result

    sent = send(pieces[0])
    squares = jnp.where(used, jnp.square(taken.astype(f32)), 0.0).reshape(owners, -1)
    facts = jnp.stack([counts, jnp.sum(squares, axis=1)], 1)
    sent = after(sent, facts, pieces[1])
    facts = exchanged(facts, (("dp", 1), ("dp", 2), ("expert", 1)))
    sent = after(sent, facts)
    facts = exchanged(after(facts, sent), (("expert", 2), ("expert", 4), ("expert", 8), ("expert", 16)))
    total = lax.dynamic_slice_in_dim(facts, lax.axis_index("expert"), 1, 0)[0]
    scale = jnp.sqrt(2.0 / total[0])[None]
    damping = (damp_share * total[1] / features)[None]
    sum_grams(sent.reshape(owners * capacity, -1), CHUNKS[0], False)
    swap_halves()
    pieces[1] = after(pieces[1], facts, swaps[0], *half_sums)
    for chunk in range(1, len(CHUNKS)):
        sent = send(after(pieces[chunk], sent))
        done = len(half_sums) - HELD[chunk]
        while len(lowers) < done:
            factor(len(lowers))
        ready = lowers[-1:]
        if len(lowers) < len(half_sums):
            ready = ready + [pair_sum(len(lowers))[0]]
        rows = after(sent, *ready)
        sum_grams(rows.reshape(owners * capacity, -1), CHUNKS[chunk], True)
        swap_halves()
    while len(lowers) < len(half_sums) - 1:
        factor(len(lowers))
    return factor(len(lowers))[None]


def solution(mesh):
    placed = (P(("dp", "expert"), None, None), P(("dp", "expert"), None))
    return jax.shard_map(
        shards, mesh=mesh, in_specs=placed, out_specs=P("expert", "dp", None), check_vma=False
    )
```

```python
import functools

import jax
import jax.numpy as jnp
from jax import lax
from jax.experimental import pallas as pl
from jax.experimental.pallas import tpu as pltpu
from jax.sharding import PartitionSpec as P

EXP_DEV = 4
WIDTH = 128
CHUNKS = ((3, 3, 2), (2, 2))
HELD = (0, 1)
damp_share = 0.01
f32 = jnp.float32
bf16 = jnp.bfloat16
VMEM = pl.BlockSpec(memory_space=pltpu.VMEM)
SMEM = pl.BlockSpec(memory_space=pltpu.SMEM)
LIMIT = pltpu.CompilerParams(vmem_limit_bytes=56 * 2**20)


def split(x):
    high = x.astype(bf16)
    rest = x - high.astype(f32)
    middle = rest.astype(bf16)
    return high, middle, (rest - middle.astype(f32)).astype(bf16)


def left_terms(x, axis=1):
    h, m, l = split(x)
    return jnp.concatenate([h, h, m, m, h, l], axis)


def right_terms(x, axis=1):
    h, m, l = split(x)
    return jnp.concatenate([h, m, h, m, l, h], axis)


def dot(a, b, contract):
    return lax.dot_general(a, b, (contract, ((), ())), preferred_element_type=f32)


def dot_nt(a, b):
    return dot(left_terms(a), right_terms(b), ((1,), (1,)))


def dot_nn(a, b):
    return dot(left_terms(a), right_terms(b, 0), ((1,), (0,)))


def over_lanes(x, j):
    return jnp.broadcast_to(x[:, j : j + 1], (8, 128))


def over_rows(x, i):
    return jnp.broadcast_to(x[i : i + 1, :], x.shape)


def eliminate(rows):
    count = len(rows)
    wide = lambda v: jnp.concatenate([v, v], axis=1)
    rows = list(rows)
    sub = lax.broadcasted_iota(jnp.int32, (8, 128), 0)
    for m in range(count):
        group = rows[m]
        cols = [over_lanes(group, 8 * m + l) for l in range(8)]
        cell = [[over_rows(cols[l], i) if i >= l else None for l in range(8)] for i in range(8)]
        below = [[over_lanes(rows[t], 8 * m + l) for l in range(8)] for t in range(m + 1, count)]
        inverse, diagonal = [], None
        ratio = [[None] * 8 for _ in range(8)]
        for j in range(8):
            d = cell[j][j]
            r = pl.reciprocal(d, approx=True)
            inverse.append(r)
            diagonal = d if diagonal is None else jnp.where(sub == j, d, diagonal)
            pairs = [(i, l) for i in range(j + 1, 8) for l in range(j + 1, i + 1)]
            products = [cell[i][j] * cell[l][j] for i, l in pairs]
            for (i, l), product in zip(pairs, products):
                cell[i][l] = cell[i][l] - product * r
            for l in range(j + 1, 8):
                ratio[l][j] = cell[l][j] * r
        pivots = []
        for j in range(8):
            pivot = over_rows(group, j)
            pivots.append(pivot)
            group = group - wide(jnp.where(sub > j, cols[j] * inverse[j], 0.0)) * pivot
            for l in range(j + 1, 8):
                cols[l] = cols[l] - cols[j] * ratio[l][j]
        rows[m] = group * wide(lax.rsqrt(diagonal))
        for b, t in zip(below, range(m + 1, count)):
            for j in range(8):
                for l in range(j + 1, 8):
                    b[l] = b[l] - b[j] * ratio[l][j]
            terms = [wide(b[j] * inverse[j]) * pivots[j] for j in range(8)]
            while len(terms) > 1:
                terms = [terms[2 * i] + terms[2 * i + 1] for i in range(len(terms) // 2)]
            rows[t] = rows[t] - terms[0]
    return rows


def identity(size):
    return (
        lax.broadcasted_iota(jnp.int32, (size, size), 0) == lax.broadcasted_iota(jnp.int32, (size, size), 1)
    ).astype(f32)


def section_kernel(bounds, here, last, share, damp_ref, *refs):
    first, end = bounds[here], bounds[here + 1]
    span = end - first
    scale_ref, spot_ref, mine_ref, other_ref = refs[:4]
    lower_refs, inverse_refs = refs[4 : 4 + here], refs[4 + here : 4 + 2 * here]
    refs = refs[4 + 2 * here :]
    if last:
        out_ref, work, tile_inverse, gram_ref, lower_ref = refs
        full_inverse = None
    else:
        lower_ref, full_inverse, work, tile_inverse, gram_ref = refs
    half = span // 2
    core = spot_ref[1]
    gram_ref[pl.ds(pl.multiple_of(core * half, half), half), :] = mine_ref[...]
    gram_ref[pl.ds(pl.multiple_of((1 - core) * half, half), half), :] = other_ref[...]
    diag = gram_ref[:, first:end] + damp_ref[0] * identity(span)
    rest = [gram_ref[:, bounds[i] : bounds[i + 1]] for i in range(here)]
    for i in range(here):
        solved = dot_nt(rest[i], inverse_refs[i][...])
        lower_ref[:, bounds[i] : bounds[i + 1]] = solved
        solved_terms = left_terms(solved)
        for n in range(i + 1, here):
            other = right_terms(lower_refs[n][:, bounds[i] : bounds[i + 1]])
            rest[n] = rest[n] - dot(solved_terms, other, ((1,), (1,)))
        diag = diag - dot(solved_terms, right_terms(solved), ((1,), (1,)))
    work[...] = diag
    eye = identity(WIDTH)
    steps = span // WIDTH

    def step(k, carry):
        start = pl.multiple_of(k * WIDTH, WIDTH)
        rows = [
            jnp.concatenate([work[pl.ds(start + t, 8), pl.ds(start, WIDTH)], eye[t : t + 8]], 1)
            for t in range(0, WIDTH, 8)
        ]
        for t, row in enumerate(eliminate(rows)):
            tile_inverse[pl.ds(start + 8 * t, 8), :] = row[:, WIDTH:]
        inverse_terms = right_terms(tile_inverse[pl.ds(start, WIDTH), :])
        for k_here in range(steps):

            @pl.when(k == k_here)
            def _(k_here=k_here):
                top = k_here * WIDTH
                below = top + WIDTH
                panel = dot(left_terms(work[top:, top:below]), inverse_terms, ((1,), (1,)))
                work[top:, top:below] = panel
                if below < span:
                    work[below:, below:] -= dot(
                        left_terms(panel[WIDTH:]), right_terms(panel[WIDTH:]), ((1,), (1,))
                    )

        return carry

    lax.fori_loop(0, steps, step, 0)
    keep = lax.broadcasted_iota(jnp.int32, (span, span), 0) >= lax.broadcasted_iota(jnp.int32, (span, span), 1)
    lower = jnp.where(keep, work[...], 0.0)
    lower_ref[:, first:end] = lower
    if full_inverse is not None:
        whole = tile_inverse[:WIDTH, :]
        for k in range(1, steps):
            top = k * WIDTH
            tile = tile_inverse[top : top + WIDTH, :]
            corner = -dot_nn(tile, dot_nn(lower[top : top + WIDTH, :top], whole))
            whole = jnp.concatenate(
                [
                    jnp.concatenate([whole, jnp.zeros((top, WIDTH), f32)], 1),
                    jnp.concatenate([corner, tile], 1),
                ],
                0,
            )
        full_inverse[...] = whole
    else:
        scale = scale_ref[0]
        place = spot_ref[0]
        sources = list(lower_refs) + [lower_ref]
        for p in range(bounds[-1] // share):

            @pl.when(place == p)
            def _(p=p):
                for i, source in enumerate(sources):
                    low, high = max(bounds[i], p * share), min(bounds[i + 1], (p + 1) * share)
                    if low < high:
                        cols = bounds[i + 1]
                        out_ref[low - p * share : high - p * share, :cols] = (
                            source[low - bounds[i] : high - bounds[i], :] * scale
                        )
                        if cols < bounds[-1]:
                            out_ref[low - p * share : high - p * share, cols:] = jnp.zeros(
                                (high - low, bounds[-1] - cols), f32
                            )


def factor_section(bounds, here, share, damping, scale, spot, mine, other, lowers, inverses):
    span = bounds[here + 1] - bounds[here]
    last = here == len(bounds) - 2
    lower_shape = jax.ShapeDtypeStruct((span, bounds[here + 1]), f32)
    scratch = [
        pltpu.VMEM((span, span), f32),
        pltpu.VMEM((span, WIDTH), f32),
        pltpu.VMEM(lower_shape.shape, f32),
    ]
    if last:
        out_shape = jax.ShapeDtypeStruct((share, bounds[-1]), f32)
        scratch.append(pltpu.VMEM(lower_shape.shape, f32))
    else:
        out_shape = (lower_shape, jax.ShapeDtypeStruct((span, span), f32))
    return pl.pallas_call(
        functools.partial(section_kernel, bounds, here, last, share),
        out_shape=out_shape,
        in_specs=[SMEM] * 3 + [VMEM] * (2 + 2 * here),
        out_specs=VMEM if last else (VMEM, VMEM),
        scratch_shapes=scratch,
        compiler_params=LIMIT,
        cost_estimate=pl.CostEstimate(flops=WIDTH * span, bytes_accessed=span, transcendentals=0),
        name="factor_section",
    )(damping, scale, spot, mine, other, *lowers, *inverses)


def route_kernel(tokens, top_k, owners, capacity, ids_ref, source_ref, count_ref):
    blocks = tokens // 128
    owner = lax.broadcasted_iota(jnp.int32, (owners, 128), 0) * EXP_DEV
    position = lax.broadcasted_iota(jnp.int32, (owners, 128), 1).astype(f32)
    slot = lax.broadcasted_iota(jnp.int32, (capacity, 128), 0).astype(f32)
    row = lax.broadcasted_iota(jnp.int32, (128, 256), 0)
    col = lax.broadcasted_iota(jnp.int32, (128, 256), 1)
    earlier_and_all = jnp.where((row < col) | (col >= 128), 1.0, 0.0).astype(bf16)
    carry = jnp.zeros((owners, 128), f32)
    found = jnp.zeros((3 * owners, capacity), f32)
    for k in range(top_k):
        chosen = [
            jnp.where(
                jnp.broadcast_to(ids_ref[k : k + 1, b * 128 : (b + 1) * 128], (owners, 128)) == owner, 1.0, 0.0
            )
            for b in range(blocks)
        ]
        sums = dot(jnp.concatenate(chosen, 0).astype(bf16), earlier_and_all, ((1,), (0,)))
        marks, slots = [], []
        for b in range(blocks):
            ones = chosen[b]
            part = sums[b * owners : (b + 1) * owners]
            rank = jnp.sum(ones * (part[:, :128] + carry), axis=0, keepdims=True)
            carry = carry + part[:, 128:]
            marks.append(jnp.concatenate([ones, ones * position, ones * float(b * top_k + k)], 0).astype(bf16))
            slots.append(jnp.where(jnp.broadcast_to(rank, (capacity, 128)) == slot, 1.0, 0.0).astype(bf16))
        found = found + dot(jnp.concatenate(marks, 1), jnp.concatenate(slots, 1), ((1,), (1,)))
    filled = found[:owners] > 0.5
    place = found[owners : 2 * owners].astype(jnp.int32)
    block = found[2 * owners :].astype(jnp.int32)
    flat = (block // top_k) * (128 * top_k) + block % top_k + place * top_k
    source_ref[...] = jnp.where(filled, flat, -1)
    count_ref[...] = carry


def route(expert_ids, owners, capacity):
    tokens, top_k = expert_ids.shape
    source, count = pl.pallas_call(
        functools.partial(route_kernel, tokens, top_k, owners, capacity),
        out_shape=(jax.ShapeDtypeStruct((owners, capacity), jnp.int32), jax.ShapeDtypeStruct((owners, 128), f32)),
        in_specs=[VMEM],
        out_specs=(VMEM, VMEM),
        compiler_params=LIMIT,
        name="route",
    )(expert_ids.T)
    return source, count[:, 0]


def swap_groups():
    groups = []
    for x_lo in range(2):
        for core in range(2):
            groups.append([(2 * (x_lo ^ (e % 2)) + core) * 32 + e for e in range(32)])
    return groups


def after(value, *others):
    return lax.optimization_barrier((value, *others))[0]


def exchanged(value, stages):
    for axis, mask in stages:
        value = value + lax.ppermute(value, axis, [(i, i ^ mask) for i in range(lax.axis_size(axis))])
    return value


def shards(hidden, expert_ids):
    tokens_here, top_k, features = hidden.shape
    owners = lax.axis_size("expert")
    parts = lax.axis_size("dp")
    share = features // parts
    capacity = 3 * tokens_here * top_k // (2 * EXP_DEV * owners)
    bounds = [0]
    for sections in CHUNKS:
        for s in sections:
            bounds.append(bounds[-1] + s * WIDTH)
    source, counts = route(expert_ids, owners, capacity)
    slots = source.reshape(-1)
    used = (slots >= 0)[:, None]
    taken = hidden.reshape(-1, features).at[jnp.maximum(slots, 0)].get(mode="promise_in_bounds")
    place = lax.axis_index("dp")
    core = place % 2
    spot = jnp.stack([place, core]).astype(jnp.int32)
    groups = swap_groups()

    pieces, low = [], 0
    for sections in CHUNKS:
        high = low + WIDTH * sum(sections)
        pieces.append(jnp.where(used, taken[:, low:high], jnp.zeros((), bf16)).reshape(owners, capacity, -1))
        low = high
    def send(piece):
        return lax.all_to_all(
            piece, ("dp", "expert"), split_axis=0, concat_axis=0, tiled=True, axis_index_groups=groups
        )

    received, half_sums, swaps, pair_sums, lowers, inverses = [], [], [], {}, [], []

    def sum_grams(rows, sections, whole):
        earlier = list(received)
        received.append(rows)
        first = sum(r.shape[1] for r in earlier)

        def gram_of(low, high):
            parts_here = [
                lax.dot_general(
                    rows[:, low:high], against, (((0,), (0,)), ((), ())), preferred_element_type=f32
                )
                for against in earlier + [rows[:, :high]]
            ]
            return jnp.concatenate(parts_here, 1) if earlier else parts_here[0]

        everything = gram_of(0, rows.shape[1]) if whole else None
        other = None
        for _ in sections:
            c = len(half_sums)
            low, high = bounds[c] - first, bounds[c + 1] - first
            if other is not None and not whole:
                rows = after(rows, other)
            gram = everything[low:high, : bounds[c + 1]] if whole else gram_of(low, high)
            half = gram.shape[0] // 2
            mine = lax.dynamic_slice_in_dim(gram, core * half, half, 0)
            other = lax.dynamic_slice_in_dim(gram, (1 - core) * half, half, 0)
            half_sums.append(mine + lax.ppermute(other, "dp", [(i, i ^ 1) for i in range(parts)]))

    def swap_halves():
        while len(swaps) < len(half_sums):
            half_sum = half_sums[len(swaps)]
            if len(swaps) == 1:
                half_sum = after(half_sum, swaps[0])
            swaps.append(lax.ppermute(half_sum, "dp", [(i, i ^ 2) for i in range(parts)]))

    def pair_sum(c):
        if c not in pair_sums:
            mine = half_sums[c] + after(swaps[c], *lowers[-1:])
            pair_sums[c] = mine, lax.ppermute(mine, "dp", [(i, i ^ 1) for i in range(parts)])
        return pair_sums[c]

    def factor(c):
        mine, other = pair_sum(c)
        mine = after(mine, *half_sums[c + 1 :])
        result = factor_section(bounds, c, share, damping, scale, spot, mine, other, lowers, inverses)
        if c < len(bounds) - 2:
            lowers.append(result[0])
            inverses.append(result[1])
        return result

    sent = send(pieces[0])
    squares = jnp.where(used, jnp.square(taken.astype(f32)), 0.0).reshape(owners, -1)
    facts = jnp.stack([counts, jnp.sum(squares, axis=1)], 1)
    sent = after(sent, facts, pieces[1])
    facts = exchanged(facts, (("dp", 1), ("dp", 2), ("expert", 1)))
    sent = after(sent, facts)
    sum_grams(sent.reshape(owners * capacity, -1), CHUNKS[0], False)
    swap_halves()
    facts = exchanged(after(facts, half_sums[0]), (("expert", 2), ("expert", 4)))
    facts = exchanged(after(facts, swaps[0]), (("expert", 8), ("expert", 16)))
    total = lax.dynamic_slice_in_dim(facts, lax.axis_index("expert"), 1, 0)[0]
    scale = jnp.sqrt(2.0 / total[0])[None]
    damping = (damp_share * total[1] / features)[None]
    pieces[1] = after(pieces[1], facts, swaps[0], *half_sums)
    for chunk in range(1, len(CHUNKS)):
        sent = send(after(pieces[chunk], sent))
        done = len(half_sums) - HELD[chunk]
        while len(lowers) < done:
            factor(len(lowers))
        ready = lowers[-1:]
        if len(lowers) < len(half_sums):
            ready = ready + [pair_sum(len(lowers))[0]]
        rows = after(sent, *ready)
        sum_grams(rows.reshape(owners * capacity, -1), CHUNKS[chunk], True)
        swap_halves()
    while len(lowers) < len(half_sums) - 1:
        factor(len(lowers))
    return factor(len(lowers))[None]


def solution(mesh):
    placed = (P(("dp", "expert"), None, None), P(("dp", "expert"), None))
    return jax.shard_map(
        shards, mesh=mesh, in_specs=placed, out_specs=P("expert", "dp", None), check_vma=False
    )
```

```python
import functools

import jax
import jax.numpy as jnp
from jax import lax
from jax.experimental import pallas as pl
from jax.experimental.pallas import tpu as pltpu
from jax.sharding import PartitionSpec as P

EXP_DEV = 4
WIDTH = 128
CHUNKS = ((3, 3, 2), (2, 2))
HELD = (0, 1)
damp_share = 0.01
f32 = jnp.float32
bf16 = jnp.bfloat16
VMEM = pl.BlockSpec(memory_space=pltpu.VMEM)
SMEM = pl.BlockSpec(memory_space=pltpu.SMEM)
LIMIT = pltpu.CompilerParams(vmem_limit_bytes=56 * 2**20)


def split(x):
    high = x.astype(bf16)
    rest = x - high.astype(f32)
    middle = rest.astype(bf16)
    return high, middle, (rest - middle.astype(f32)).astype(bf16)


def left_terms(x, axis=1):
    h, m, l = split(x)
    return jnp.concatenate([h, h, m, m, h, l], axis)


def right_terms(x, axis=1):
    h, m, l = split(x)
    return jnp.concatenate([h, m, h, m, l, h], axis)


def dot(a, b, contract):
    return lax.dot_general(a, b, (contract, ((), ())), preferred_element_type=f32)


def dot_nt(a, b):
    return dot(left_terms(a), right_terms(b), ((1,), (1,)))


def dot_nn(a, b):
    return dot(left_terms(a), right_terms(b, 0), ((1,), (0,)))


def over_lanes(x, j):
    return jnp.broadcast_to(x[:, j : j + 1], (8, 128))


def over_rows(x, i):
    return jnp.broadcast_to(x[i : i + 1, :], x.shape)


def eliminate(rows):
    count = len(rows)
    wide = lambda v: jnp.concatenate([v, v], axis=1)
    rows = list(rows)
    sub = lax.broadcasted_iota(jnp.int32, (8, 128), 0)
    for m in range(count):
        group = rows[m]
        cols = [over_lanes(group, 8 * m + l) for l in range(8)]
        cell = [[over_rows(cols[l], i) if i >= l else None for l in range(8)] for i in range(8)]
        below = [[over_lanes(rows[t], 8 * m + l) for l in range(8)] for t in range(m + 1, count)]
        inverse, diagonal = [], None
        ratio = [[None] * 8 for _ in range(8)]
        for j in range(8):
            d = cell[j][j]
            r = pl.reciprocal(d, approx=True)
            inverse.append(r)
            diagonal = d if diagonal is None else jnp.where(sub == j, d, diagonal)
            pairs = [(i, l) for i in range(j + 1, 8) for l in range(j + 1, i + 1)]
            products = [cell[i][j] * cell[l][j] for i, l in pairs]
            for (i, l), product in zip(pairs, products):
                cell[i][l] = cell[i][l] - product * r
            for l in range(j + 1, 8):
                ratio[l][j] = cell[l][j] * r
        pivots = []
        for j in range(8):
            pivot = over_rows(group, j)
            pivots.append(pivot)
            group = group - wide(jnp.where(sub > j, cols[j] * inverse[j], 0.0)) * pivot
            for l in range(j + 1, 8):
                cols[l] = cols[l] - cols[j] * ratio[l][j]
        rows[m] = group * wide(lax.rsqrt(diagonal))
        for b, t in zip(below, range(m + 1, count)):
            for j in range(8):
                for l in range(j + 1, 8):
                    b[l] = b[l] - b[j] * ratio[l][j]
            terms = [wide(b[j] * inverse[j]) * pivots[j] for j in range(8)]
            while len(terms) > 1:
                terms = [terms[2 * i] + terms[2 * i + 1] for i in range(len(terms) // 2)]
            rows[t] = rows[t] - terms[0]
    return rows


def identity(size):
    return (
        lax.broadcasted_iota(jnp.int32, (size, size), 0) == lax.broadcasted_iota(jnp.int32, (size, size), 1)
    ).astype(f32)


def section_kernel(bounds, here, last, share, damp_ref, *refs):
    first, end = bounds[here], bounds[here + 1]
    span = end - first
    scale_ref, spot_ref, mine_ref, other_ref = refs[:4]
    lower_refs, inverse_refs = refs[4 : 4 + here], refs[4 + here : 4 + 2 * here]
    refs = refs[4 + 2 * here :]
    if last:
        out_ref, work, tile_inverse, gram_ref, lower_ref = refs
        full_inverse = None
    else:
        lower_ref, full_inverse, work, tile_inverse, gram_ref = refs
    half = span // 2
    core = spot_ref[1]
    gram_ref[pl.ds(pl.multiple_of(core * half, half), half), :] = mine_ref[...]
    gram_ref[pl.ds(pl.multiple_of((1 - core) * half, half), half), :] = other_ref[...]
    diag = gram_ref[:, first:end] + damp_ref[0] * identity(span)
    rest = [gram_ref[:, bounds[i] : bounds[i + 1]] for i in range(here)]
    for i in range(here):
        solved = dot_nt(rest[i], inverse_refs[i][...])
        lower_ref[:, bounds[i] : bounds[i + 1]] = solved
        solved_terms = left_terms(solved)
        for n in range(i + 1, here):
            other = right_terms(lower_refs[n][:, bounds[i] : bounds[i + 1]])
            rest[n] = rest[n] - dot(solved_terms, other, ((1,), (1,)))
        diag = diag - dot(solved_terms, right_terms(solved), ((1,), (1,)))
    work[...] = diag
    eye = identity(WIDTH)
    steps = span // WIDTH

    def step(k, carry):
        start = pl.multiple_of(k * WIDTH, WIDTH)
        rows = [
            jnp.concatenate([work[pl.ds(start + t, 8), pl.ds(start, WIDTH)], eye[t : t + 8]], 1)
            for t in range(0, WIDTH, 8)
        ]
        for t, row in enumerate(eliminate(rows)):
            tile_inverse[pl.ds(start + 8 * t, 8), :] = row[:, WIDTH:]
        inverse_terms = right_terms(tile_inverse[pl.ds(start, WIDTH), :])
        for k_here in range(steps):

            @pl.when(k == k_here)
            def _(k_here=k_here):
                top = k_here * WIDTH
                below = top + WIDTH
                panel = dot(left_terms(work[top:, top:below]), inverse_terms, ((1,), (1,)))
                work[top:, top:below] = panel
                if below < span:
                    work[below:, below:] -= dot(
                        left_terms(panel[WIDTH:]), right_terms(panel[WIDTH:]), ((1,), (1,))
                    )

        return carry

    lax.fori_loop(0, steps, step, 0)
    keep = lax.broadcasted_iota(jnp.int32, (span, span), 0) >= lax.broadcasted_iota(jnp.int32, (span, span), 1)
    lower = jnp.where(keep, work[...], 0.0)
    lower_ref[:, first:end] = lower
    if full_inverse is not None:
        whole = tile_inverse[:WIDTH, :]
        for k in range(1, steps):
            top = k * WIDTH
            tile = tile_inverse[top : top + WIDTH, :]
            corner = -dot_nn(tile, dot_nn(lower[top : top + WIDTH, :top], whole))
            whole = jnp.concatenate(
                [
                    jnp.concatenate([whole, jnp.zeros((top, WIDTH), f32)], 1),
                    jnp.concatenate([corner, tile], 1),
                ],
                0,
            )
        full_inverse[...] = whole
    else:
        scale = scale_ref[0]
        place = spot_ref[0]
        sources = list(lower_refs) + [lower_ref]
        for p in range(bounds[-1] // share):

            @pl.when(place == p)
            def _(p=p):
                for i, source in enumerate(sources):
                    low, high = max(bounds[i], p * share), min(bounds[i + 1], (p + 1) * share)
                    if low < high:
                        cols = bounds[i + 1]
                        out_ref[low - p * share : high - p * share, :cols] = (
                            source[low - bounds[i] : high - bounds[i], :] * scale
                        )
                        if cols < bounds[-1]:
                            out_ref[low - p * share : high - p * share, cols:] = jnp.zeros(
                                (high - low, bounds[-1] - cols), f32
                            )


def factor_section(bounds, here, share, damping, scale, spot, mine, other, lowers, inverses):
    span = bounds[here + 1] - bounds[here]
    last = here == len(bounds) - 2
    lower_shape = jax.ShapeDtypeStruct((span, bounds[here + 1]), f32)
    scratch = [
        pltpu.VMEM((span, span), f32),
        pltpu.VMEM((span, WIDTH), f32),
        pltpu.VMEM(lower_shape.shape, f32),
    ]
    if last:
        out_shape = jax.ShapeDtypeStruct((share, bounds[-1]), f32)
        scratch.append(pltpu.VMEM(lower_shape.shape, f32))
    else:
        out_shape = (lower_shape, jax.ShapeDtypeStruct((span, span), f32))
    return pl.pallas_call(
        functools.partial(section_kernel, bounds, here, last, share),
        out_shape=out_shape,
        in_specs=[SMEM] * 3 + [VMEM] * (2 + 2 * here),
        out_specs=VMEM if last else (VMEM, VMEM),
        scratch_shapes=scratch,
        compiler_params=LIMIT,
        cost_estimate=pl.CostEstimate(flops=WIDTH * span, bytes_accessed=span, transcendentals=0),
        name="factor_section",
    )(damping, scale, spot, mine, other, *lowers, *inverses)


def route_kernel(tokens, top_k, owners, capacity, ids_ref, source_ref, count_ref):
    blocks = tokens // 128
    owner = lax.broadcasted_iota(jnp.int32, (owners, 128), 0) * EXP_DEV
    position = lax.broadcasted_iota(jnp.int32, (owners, 128), 1).astype(f32)
    slot = lax.broadcasted_iota(jnp.int32, (capacity, 128), 0).astype(f32)
    row = lax.broadcasted_iota(jnp.int32, (128, 256), 0)
    col = lax.broadcasted_iota(jnp.int32, (128, 256), 1)
    earlier_and_all = jnp.where((row < col) | (col >= 128), 1.0, 0.0).astype(bf16)
    carry = jnp.zeros((owners, 128), f32)
    found = jnp.zeros((3 * owners, capacity), f32)
    for k in range(top_k):
        chosen = [
            jnp.where(
                jnp.broadcast_to(ids_ref[k : k + 1, b * 128 : (b + 1) * 128], (owners, 128)) == owner, 1.0, 0.0
            )
            for b in range(blocks)
        ]
        sums = dot(jnp.concatenate(chosen, 0).astype(bf16), earlier_and_all, ((1,), (0,)))
        marks, slots = [], []
        for b in range(blocks):
            ones = chosen[b]
            part = sums[b * owners : (b + 1) * owners]
            rank = jnp.sum(ones * (part[:, :128] + carry), axis=0, keepdims=True)
            carry = carry + part[:, 128:]
            marks.append(jnp.concatenate([ones, ones * position, ones * float(b * top_k + k)], 0).astype(bf16))
            slots.append(jnp.where(jnp.broadcast_to(rank, (capacity, 128)) == slot, 1.0, 0.0).astype(bf16))
        found = found + dot(jnp.concatenate(marks, 1), jnp.concatenate(slots, 1), ((1,), (1,)))
    filled = found[:owners] > 0.5
    place = found[owners : 2 * owners].astype(jnp.int32)
    block = found[2 * owners :].astype(jnp.int32)
    flat = (block // top_k) * (128 * top_k) + block % top_k + place * top_k
    source_ref[...] = jnp.where(filled, flat, -1)
    count_ref[...] = carry


def route(expert_ids, owners, capacity):
    tokens, top_k = expert_ids.shape
    source, count = pl.pallas_call(
        functools.partial(route_kernel, tokens, top_k, owners, capacity),
        out_shape=(jax.ShapeDtypeStruct((owners, capacity), jnp.int32), jax.ShapeDtypeStruct((owners, 128), f32)),
        in_specs=[VMEM],
        out_specs=(VMEM, VMEM),
        compiler_params=LIMIT,
        name="route",
    )(expert_ids.T)
    return source, count[:, 0]


def swap_groups():
    groups = []
    for x_lo in range(2):
        for core in range(2):
            groups.append([(2 * (x_lo ^ (e % 2)) + core) * 32 + e for e in range(32)])
    return groups


def after(value, *others):
    return lax.optimization_barrier((value, *others))[0]


def exchanged(value, stages):
    for axis, mask in stages:
        value = value + lax.ppermute(value, axis, [(i, i ^ mask) for i in range(lax.axis_size(axis))])
    return value


def shards(hidden, expert_ids):
    tokens_here, top_k, features = hidden.shape
    owners = lax.axis_size("expert")
    parts = lax.axis_size("dp")
    share = features // parts
    capacity = 3 * tokens_here * top_k // (2 * EXP_DEV * owners)
    bounds = [0]
    for sections in CHUNKS:
        for s in sections:
            bounds.append(bounds[-1] + s * WIDTH)
    source, counts = route(expert_ids, owners, capacity)
    slots = source.reshape(-1)
    used = (slots >= 0)[:, None]
    taken = hidden.reshape(-1, features).at[jnp.maximum(slots, 0)].get(mode="promise_in_bounds")
    place = lax.axis_index("dp")
    core = place % 2
    spot = jnp.stack([place, core]).astype(jnp.int32)
    groups = swap_groups()

    pieces, low = [], 0
    for sections in CHUNKS:
        high = low + WIDTH * sum(sections)
        pieces.append(jnp.where(used, taken[:, low:high], jnp.zeros((), bf16)).reshape(owners, capacity, -1))
        low = high
    def send(piece):
        return lax.all_to_all(
            piece, ("dp", "expert"), split_axis=0, concat_axis=0, tiled=True, axis_index_groups=groups
        )

    received, half_sums, swaps, pair_sums, lowers, inverses = [], [], [], {}, [], []

    def sum_grams(rows, sections, whole):
        earlier = list(received)
        received.append(rows)
        first = sum(r.shape[1] for r in earlier)

        def gram_of(low, high):
            parts_here = [
                lax.dot_general(
                    rows[:, low:high], against, (((0,), (0,)), ((), ())), preferred_element_type=f32
                )
                for against in earlier + [rows[:, :high]]
            ]
            return jnp.concatenate(parts_here, 1) if earlier else parts_here[0]

        everything = gram_of(0, rows.shape[1]) if whole else None
        other = None
        for _ in sections:
            c = len(half_sums)
            low, high = bounds[c] - first, bounds[c + 1] - first
            if other is not None and not whole:
                rows = after(rows, other)
            gram = everything[low:high, : bounds[c + 1]] if whole else gram_of(low, high)
            half = gram.shape[0] // 2
            mine = lax.dynamic_slice_in_dim(gram, core * half, half, 0)
            other = lax.dynamic_slice_in_dim(gram, (1 - core) * half, half, 0)
            half_sums.append(mine + lax.ppermute(other, "dp", [(i, i ^ 1) for i in range(parts)]))

    def swap_halves():
        while len(swaps) < len(half_sums):
            half_sum = half_sums[len(swaps)]
            if len(swaps) == 1:
                half_sum = after(half_sum, swaps[0])
            swaps.append(lax.ppermute(half_sum, "dp", [(i, i ^ 2) for i in range(parts)]))

    def pair_sum(c):
        if c not in pair_sums:
            mine = half_sums[c] + after(swaps[c], *lowers[-1:])
            pair_sums[c] = mine, lax.ppermute(mine, "dp", [(i, i ^ 1) for i in range(parts)])
        return pair_sums[c]

    def factor(c):
        mine, other = pair_sum(c)
        mine = after(mine, *half_sums[c + 1 :])
        result = factor_section(bounds, c, share, damping, scale, spot, mine, other, lowers, inverses)
        if c < len(bounds) - 2:
            lowers.append(result[0])
            inverses.append(result[1])
        return result

    sent = send(pieces[0])
    squares = jnp.where(used, jnp.square(taken.astype(f32)), 0.0).reshape(owners, -1)
    facts = jnp.stack([counts, jnp.sum(squares, axis=1)], 1)
    sent = after(sent, facts, pieces[1])
    facts = exchanged(facts, [("dp", m) for m in (1, 2)] + [("expert", m) for m in (1, 2, 4, 8, 16)])
    sent = after(sent, facts)
    sum_grams(sent.reshape(owners * capacity, -1), CHUNKS[0], False)
    swap_halves()
    total = lax.dynamic_slice_in_dim(facts, lax.axis_index("expert"), 1, 0)[0]
    scale = jnp.sqrt(2.0 / total[0])[None]
    damping = (damp_share * total[1] / features)[None]
    pieces[1] = after(pieces[1], swaps[0], *half_sums)
    for chunk in range(1, len(CHUNKS)):
        sent = send(after(pieces[chunk], sent))
        done = len(half_sums) - HELD[chunk]
        while len(lowers) < done:
            factor(len(lowers))
        ready = lowers[-1:]
        if len(lowers) < len(half_sums):
            ready = ready + [pair_sum(len(lowers))[0]]
        rows = after(sent, *ready)
        sum_grams(rows.reshape(owners * capacity, -1), CHUNKS[chunk], True)
        swap_halves()
    while len(lowers) < len(half_sums) - 1:
        factor(len(lowers))
    return factor(len(lowers))[None]


def solution(mesh):
    placed = (P(("dp", "expert"), None, None), P(("dp", "expert"), None))
    return jax.shard_map(
        shards, mesh=mesh, in_specs=placed, out_specs=P("expert", "dp", None), check_vma=False
    )
```

```python
import functools

import jax
import jax.numpy as jnp
from jax import lax
from jax.experimental import pallas as pl
from jax.experimental.pallas import tpu as pltpu
from jax.sharding import PartitionSpec as P

EXP_DEV = 4
WIDTH = 128
CHUNKS = ((3, 2, 2), (2, 3))
HELD = (0, 1)
damp_share = 0.01
f32 = jnp.float32
bf16 = jnp.bfloat16
VMEM = pl.BlockSpec(memory_space=pltpu.VMEM)
SMEM = pl.BlockSpec(memory_space=pltpu.SMEM)
LIMIT = pltpu.CompilerParams(vmem_limit_bytes=56 * 2**20)


def split(x):
    high = x.astype(bf16)
    rest = x - high.astype(f32)
    middle = rest.astype(bf16)
    return high, middle, (rest - middle.astype(f32)).astype(bf16)


def left_terms(x, axis=1):
    h, m, l = split(x)
    return jnp.concatenate([h, h, m, m, h, l], axis)


def right_terms(x, axis=1):
    h, m, l = split(x)
    return jnp.concatenate([h, m, h, m, l, h], axis)


def dot(a, b, contract):
    return lax.dot_general(a, b, (contract, ((), ())), preferred_element_type=f32)


def dot_nt(a, b):
    return dot(left_terms(a), right_terms(b), ((1,), (1,)))


def dot_nn(a, b):
    return dot(left_terms(a), right_terms(b, 0), ((1,), (0,)))


def over_lanes(x, j):
    return jnp.broadcast_to(x[:, j : j + 1], (8, 128))


def over_rows(x, i):
    return jnp.broadcast_to(x[i : i + 1, :], x.shape)


def eliminate(rows):
    count = len(rows)
    wide = lambda v: jnp.concatenate([v, v], axis=1)
    rows = list(rows)
    sub = lax.broadcasted_iota(jnp.int32, (8, 128), 0)
    for m in range(count):
        group = rows[m]
        cols = [over_lanes(group, 8 * m + l) for l in range(8)]
        cell = [[over_rows(cols[l], i) if i >= l else None for l in range(8)] for i in range(8)]
        below = [[over_lanes(rows[t], 8 * m + l) for l in range(8)] for t in range(m + 1, count)]
        inverse, diagonal = [], None
        ratio = [[None] * 8 for _ in range(8)]
        for j in range(8):
            d = cell[j][j]
            r = pl.reciprocal(d, approx=True)
            inverse.append(r)
            diagonal = d if diagonal is None else jnp.where(sub == j, d, diagonal)
            pairs = [(i, l) for i in range(j + 1, 8) for l in range(j + 1, i + 1)]
            products = [cell[i][j] * cell[l][j] for i, l in pairs]
            for (i, l), product in zip(pairs, products):
                cell[i][l] = cell[i][l] - product * r
            for l in range(j + 1, 8):
                ratio[l][j] = cell[l][j] * r
        pivots = []
        for j in range(8):
            pivot = over_rows(group, j)
            pivots.append(pivot)
            group = group - wide(jnp.where(sub > j, cols[j] * inverse[j], 0.0)) * pivot
            for l in range(j + 1, 8):
                cols[l] = cols[l] - cols[j] * ratio[l][j]
        rows[m] = group * wide(lax.rsqrt(diagonal))
        for b, t in zip(below, range(m + 1, count)):
            for j in range(8):
                for l in range(j + 1, 8):
                    b[l] = b[l] - b[j] * ratio[l][j]
            terms = [wide(b[j] * inverse[j]) * pivots[j] for j in range(8)]
            while len(terms) > 1:
                terms = [terms[2 * i] + terms[2 * i + 1] for i in range(len(terms) // 2)]
            rows[t] = rows[t] - terms[0]
    return rows


def identity(size):
    return (
        lax.broadcasted_iota(jnp.int32, (size, size), 0) == lax.broadcasted_iota(jnp.int32, (size, size), 1)
    ).astype(f32)


def section_kernel(bounds, here, last, share, damp_ref, *refs):
    first, end = bounds[here], bounds[here + 1]
    span = end - first
    scale_ref, spot_ref, mine_ref, other_ref = refs[:4]
    lower_refs, inverse_refs = refs[4 : 4 + here], refs[4 + here : 4 + 2 * here]
    refs = refs[4 + 2 * here :]
    if last:
        out_ref, work, tile_inverse, gram_ref, lower_ref = refs
        full_inverse = None
    else:
        lower_ref, full_inverse, work, tile_inverse, gram_ref = refs
    half = span // 2
    core = spot_ref[1]
    gram_ref[pl.ds(pl.multiple_of(core * half, half), half), :] = mine_ref[...]
    gram_ref[pl.ds(pl.multiple_of((1 - core) * half, half), half), :] = other_ref[...]
    diag = gram_ref[:, first:end] + damp_ref[0] * identity(span)
    rest = [gram_ref[:, bounds[i] : bounds[i + 1]] for i in range(here)]
    for i in range(here):
        solved = dot_nt(rest[i], inverse_refs[i][...])
        lower_ref[:, bounds[i] : bounds[i + 1]] = solved
        solved_terms = left_terms(solved)
        for n in range(i + 1, here):
            other = right_terms(lower_refs[n][:, bounds[i] : bounds[i + 1]])
            rest[n] = rest[n] - dot(solved_terms, other, ((1,), (1,)))
        diag = diag - dot(solved_terms, right_terms(solved), ((1,), (1,)))
    work[...] = diag
    eye = identity(WIDTH)
    steps = span // WIDTH

    def step(k, carry):
        start = pl.multiple_of(k * WIDTH, WIDTH)
        rows = [
            jnp.concatenate([work[pl.ds(start + t, 8), pl.ds(start, WIDTH)], eye[t : t + 8]], 1)
            for t in range(0, WIDTH, 8)
        ]
        for t, row in enumerate(eliminate(rows)):
            tile_inverse[pl.ds(start + 8 * t, 8), :] = row[:, WIDTH:]
        inverse_terms = right_terms(tile_inverse[pl.ds(start, WIDTH), :])
        for k_here in range(steps):

            @pl.when(k == k_here)
            def _(k_here=k_here):
                top = k_here * WIDTH
                below = top + WIDTH
                panel = dot(left_terms(work[top:, top:below]), inverse_terms, ((1,), (1,)))
                work[top:, top:below] = panel
                if below < span:
                    work[below:, below:] -= dot(
                        left_terms(panel[WIDTH:]), right_terms(panel[WIDTH:]), ((1,), (1,))
                    )

        return carry

    lax.fori_loop(0, steps, step, 0)
    keep = lax.broadcasted_iota(jnp.int32, (span, span), 0) >= lax.broadcasted_iota(jnp.int32, (span, span), 1)
    lower = jnp.where(keep, work[...], 0.0)
    lower_ref[:, first:end] = lower
    if full_inverse is not None:
        whole = tile_inverse[:WIDTH, :]
        for k in range(1, steps):
            top = k * WIDTH
            tile = tile_inverse[top : top + WIDTH, :]
            corner = -dot_nn(tile, dot_nn(lower[top : top + WIDTH, :top], whole))
            whole = jnp.concatenate(
                [
                    jnp.concatenate([whole, jnp.zeros((top, WIDTH), f32)], 1),
                    jnp.concatenate([corner, tile], 1),
                ],
                0,
            )
        full_inverse[...] = whole
    else:
        scale = scale_ref[0]
        place = spot_ref[0]
        sources = list(lower_refs) + [lower_ref]
        for p in range(bounds[-1] // share):

            @pl.when(place == p)
            def _(p=p):
                for i, source in enumerate(sources):
                    low, high = max(bounds[i], p * share), min(bounds[i + 1], (p + 1) * share)
                    if low < high:
                        cols = bounds[i + 1]
                        out_ref[low - p * share : high - p * share, :cols] = (
                            source[low - bounds[i] : high - bounds[i], :] * scale
                        )
                        if cols < bounds[-1]:
                            out_ref[low - p * share : high - p * share, cols:] = jnp.zeros(
                                (high - low, bounds[-1] - cols), f32
                            )


def factor_section(bounds, here, share, damping, scale, spot, mine, other, lowers, inverses):
    span = bounds[here + 1] - bounds[here]
    last = here == len(bounds) - 2
    lower_shape = jax.ShapeDtypeStruct((span, bounds[here + 1]), f32)
    scratch = [
        pltpu.VMEM((span, span), f32),
        pltpu.VMEM((span, WIDTH), f32),
        pltpu.VMEM(lower_shape.shape, f32),
    ]
    if last:
        out_shape = jax.ShapeDtypeStruct((share, bounds[-1]), f32)
        scratch.append(pltpu.VMEM(lower_shape.shape, f32))
    else:
        out_shape = (lower_shape, jax.ShapeDtypeStruct((span, span), f32))
    return pl.pallas_call(
        functools.partial(section_kernel, bounds, here, last, share),
        out_shape=out_shape,
        in_specs=[SMEM] * 3 + [VMEM] * (2 + 2 * here),
        out_specs=VMEM if last else (VMEM, VMEM),
        scratch_shapes=scratch,
        compiler_params=LIMIT,
        cost_estimate=pl.CostEstimate(flops=WIDTH * span, bytes_accessed=span, transcendentals=0),
        name="factor_section",
    )(damping, scale, spot, mine, other, *lowers, *inverses)


def route_kernel(tokens, top_k, owners, capacity, ids_ref, source_ref, count_ref):
    blocks = tokens // 128
    owner = lax.broadcasted_iota(jnp.int32, (owners, 128), 0) * EXP_DEV
    position = lax.broadcasted_iota(jnp.int32, (owners, 128), 1).astype(f32)
    slot = lax.broadcasted_iota(jnp.int32, (capacity, 128), 0).astype(f32)
    row = lax.broadcasted_iota(jnp.int32, (128, 256), 0)
    col = lax.broadcasted_iota(jnp.int32, (128, 256), 1)
    earlier_and_all = jnp.where((row < col) | (col >= 128), 1.0, 0.0).astype(bf16)
    carry = jnp.zeros((owners, 128), f32)
    found = jnp.zeros((3 * owners, capacity), f32)
    for k in range(top_k):
        chosen = [
            jnp.where(
                jnp.broadcast_to(ids_ref[k : k + 1, b * 128 : (b + 1) * 128], (owners, 128)) == owner, 1.0, 0.0
            )
            for b in range(blocks)
        ]
        sums = dot(jnp.concatenate(chosen, 0).astype(bf16), earlier_and_all, ((1,), (0,)))
        marks, slots = [], []
        for b in range(blocks):
            ones = chosen[b]
            part = sums[b * owners : (b + 1) * owners]
            rank = jnp.sum(ones * (part[:, :128] + carry), axis=0, keepdims=True)
            carry = carry + part[:, 128:]
            marks.append(jnp.concatenate([ones, ones * position, ones * float(b * top_k + k)], 0).astype(bf16))
            slots.append(jnp.where(jnp.broadcast_to(rank, (capacity, 128)) == slot, 1.0, 0.0).astype(bf16))
        found = found + dot(jnp.concatenate(marks, 1), jnp.concatenate(slots, 1), ((1,), (1,)))
    filled = found[:owners] > 0.5
    place = found[owners : 2 * owners].astype(jnp.int32)
    block = found[2 * owners :].astype(jnp.int32)
    flat = (block // top_k) * (128 * top_k) + block % top_k + place * top_k
    source_ref[...] = jnp.where(filled, flat, -1)
    count_ref[...] = carry


def route(expert_ids, owners, capacity):
    tokens, top_k = expert_ids.shape
    source, count = pl.pallas_call(
        functools.partial(route_kernel, tokens, top_k, owners, capacity),
        out_shape=(jax.ShapeDtypeStruct((owners, capacity), jnp.int32), jax.ShapeDtypeStruct((owners, 128), f32)),
        in_specs=[VMEM],
        out_specs=(VMEM, VMEM),
        compiler_params=LIMIT,
        name="route",
    )(expert_ids.T)
    return source, count[:, 0]


def swap_groups():
    groups = []
    for x_lo in range(2):
        for core in range(2):
            groups.append([(2 * (x_lo ^ (e % 2)) + core) * 32 + e for e in range(32)])
    return groups


def after(value, *others):
    return lax.optimization_barrier((value, *others))[0]


def exchanged(value, stages):
    for axis, mask in stages:
        value = value + lax.ppermute(value, axis, [(i, i ^ mask) for i in range(lax.axis_size(axis))])
    return value


def shards(hidden, expert_ids):
    tokens_here, top_k, features = hidden.shape
    owners = lax.axis_size("expert")
    parts = lax.axis_size("dp")
    share = features // parts
    capacity = 3 * tokens_here * top_k // (2 * EXP_DEV * owners)
    bounds = [0]
    for sections in CHUNKS:
        for s in sections:
            bounds.append(bounds[-1] + s * WIDTH)
    source, counts = route(expert_ids, owners, capacity)
    slots = source.reshape(-1)
    used = (slots >= 0)[:, None]
    taken = hidden.reshape(-1, features).at[jnp.maximum(slots, 0)].get(mode="promise_in_bounds")
    place = lax.axis_index("dp")
    core = place % 2
    spot = jnp.stack([place, core]).astype(jnp.int32)
    groups = swap_groups()

    pieces, low = [], 0
    for sections in CHUNKS:
        high = low + WIDTH * sum(sections)
        pieces.append(jnp.where(used, taken[:, low:high], jnp.zeros((), bf16)).reshape(owners, capacity, -1))
        low = high
    def send(piece):
        return lax.all_to_all(
            piece, ("dp", "expert"), split_axis=0, concat_axis=0, tiled=True, axis_index_groups=groups
        )

    received, half_sums, swaps, pair_sums, lowers, inverses = [], [], [], {}, [], []

    def sum_grams(rows, sections, whole):
        earlier = list(received)
        received.append(rows)
        first = sum(r.shape[1] for r in earlier)

        def gram_of(low, high):
            parts_here = [
                lax.dot_general(
                    rows[:, low:high], against, (((0,), (0,)), ((), ())), preferred_element_type=f32
                )
                for against in earlier + [rows[:, :high]]
            ]
            return jnp.concatenate(parts_here, 1) if earlier else parts_here[0]

        everything = gram_of(0, rows.shape[1]) if whole else None
        other = None
        for _ in sections:
            c = len(half_sums)
            low, high = bounds[c] - first, bounds[c + 1] - first
            if other is not None and not whole:
                rows = after(rows, other)
            gram = everything[low:high, : bounds[c + 1]] if whole else gram_of(low, high)
            half = gram.shape[0] // 2
            mine = lax.dynamic_slice_in_dim(gram, core * half, half, 0)
            other = lax.dynamic_slice_in_dim(gram, (1 - core) * half, half, 0)
            half_sums.append(mine + lax.ppermute(other, "dp", [(i, i ^ 1) for i in range(parts)]))

    def swap_halves():
        while len(swaps) < len(half_sums):
            half_sum = half_sums[len(swaps)]
            if len(swaps) == 1:
                half_sum = after(half_sum, swaps[0])
            swaps.append(lax.ppermute(half_sum, "dp", [(i, i ^ 2) for i in range(parts)]))

    def pair_sum(c):
        if c not in pair_sums:
            mine = half_sums[c] + after(swaps[c], *lowers[-1:])
            pair_sums[c] = mine, lax.ppermute(mine, "dp", [(i, i ^ 1) for i in range(parts)])
        return pair_sums[c]

    def factor(c):
        mine, other = pair_sum(c)
        mine = after(mine, *half_sums[c + 1 :])
        result = factor_section(bounds, c, share, damping, scale, spot, mine, other, lowers, inverses)
        if c < len(bounds) - 2:
            lowers.append(result[0])
            inverses.append(result[1])
        return result

    sent = send(pieces[0])
    squares = jnp.where(used, jnp.square(taken.astype(f32)), 0.0).reshape(owners, -1)
    facts = jnp.stack([counts, jnp.sum(squares, axis=1)], 1)
    sent = after(sent, facts, pieces[1])
    facts = exchanged(facts, [("dp", m) for m in (1, 2)] + [("expert", m) for m in (1, 2, 4, 8, 16)])
    sent = after(sent, facts)
    sum_grams(sent.reshape(owners * capacity, -1), CHUNKS[0], False)
    swap_halves()
    total = lax.dynamic_slice_in_dim(facts, lax.axis_index("expert"), 1, 0)[0]
    scale = jnp.sqrt(2.0 / total[0])[None]
    damping = (damp_share * total[1] / features)[None]
    pieces[1] = after(pieces[1], swaps[0], *half_sums)
    for chunk in range(1, len(CHUNKS)):
        sent = send(after(pieces[chunk], sent))
        done = len(half_sums) - HELD[chunk]
        while len(lowers) < done:
            factor(len(lowers))
        ready = lowers[-1:]
        if len(lowers) < len(half_sums):
            ready = ready + [pair_sum(len(lowers))[0]]
        rows = after(sent, *ready)
        sum_grams(rows.reshape(owners * capacity, -1), CHUNKS[chunk], True)
        swap_halves()
    while len(lowers) < len(half_sums) - 1:
        factor(len(lowers))
    return factor(len(lowers))[None]


def solution(mesh):
    placed = (P(("dp", "expert"), None, None), P(("dp", "expert"), None))
    return jax.shard_map(
        shards, mesh=mesh, in_specs=placed, out_specs=P("expert", "dp", None), check_vma=False
    )
```
